128 devices in a mesh: dp: 8 (over y, core), tensor: 16 (over z, x).
Axes of the slice: x: 4, y: 4, z: 4, core: 2. Of those that a mesh axis runs over, the one named last changes fastest.
Arguments:
- patches: bfloat16 [8, 2048, 3072], P('dp', 'tensor'), may hold values from -600 to 600
- counts: int32 [8, 16], P('dp'), may hold values from 0 to 256, as said below
- norm_gain: float32 [3072], replicated, may hold values from 0.5 to 1.5
- norm_bias: float32 [3072], replicated, may hold values from -3 to 3
- qkv_weight: bfloat16 [3072, 3, 4096], P(None, None, 'tensor'), may hold values from -0.109375 to 0.109375
- query_gain: float32 [4096], P('tensor'), may hold values from 0.1 to 1.9
- key_gain: float32 [4096], P('tensor'), may hold values from 0.1 to 1.9
- upstream: bfloat16 [8, 2048, 4096], P('dp', None, 'tensor'), may hold values from -30 to 30
Outputs:
- attention: bfloat16 [8, 2048, 4096], P('dp', None, 'tensor')
- patch_grad: bfloat16 [8, 2048, 3072], P('dp', 'tensor')
- weight_grad: float32 [3072, 3, 4096], P('dp', None, 'tensor')
- gain_grad: float32 [3072], replicated
- shift_grad: float32 [3072], replicated
- qnorm_grad: float32 [4096], P('tensor')
- knorm_grad: float32 [4096], P('tensor')
The draws below stay inside these ranges and needn't reach their ends.
Inputs may be any that keep to these rules, and one draw needn't show every extreme that they name: `counts`: for each group and each aligned pair of slots 2p, 2p + 1: either slot 2p holds more than 128 patches and slot 2p + 1 holds 0, or both hold 1 to 128. The image of slot j begins at row j * 128 of its sequence; rows past its count are padding. Every group has an image of 256 patches.
All inputs are finite; a program needn't handle non-finite values.
Results may differ from the reference program's by a relative error of at most 0.014.
Values may be sent and summed in bfloat16 or wider, within the bound.
No kernel may reach another device: no remote copies, remote signals or barrier semaphores. Data moves between devices by JAX's collectives and lax.ppermute only.
A program may use at most 192 MiB of HBM per device.

```python
import math
import jax
import jax.numpy as jnp
from jax import lax

D = 3072
HEADS = 32
HDIM = 128
BLK = 128
ABLK = 512
SEQ = 2048
N_DP = 8


def draw_patches(key, part):
    key = jax.random.fold_in(key, 11)
    keys = jax.random.split(key, 3)
    column = jnp.exp(jax.random.uniform(keys[1], (D,), jnp.float32, 0.0, math.log(10.0)))
    row = jnp.exp(jax.random.uniform(keys[2], (N_DP, SEQ, 1), jnp.float32, 0.0, math.log(10.0)))
    base = jax.random.normal(keys[0], (N_DP, SEQ, D), jnp.float32)
    return (base * column * row).astype(jnp.bfloat16)


def draw_counts(key, part):
    key = jax.random.fold_in(key, 23)
    keys = jax.random.split(key, 4)
    pairs = SEQ // BLK // 2
    merged = jax.random.randint(keys[0], (N_DP, pairs), 0, 2)
    forced = jax.random.randint(keys[1], (N_DP, 1), 0, pairs)
    hit = jnp.arange(pairs, dtype=jnp.int32)[None, :] == forced
    merged = jnp.where(hit, 1, merged)
    large = jax.random.randint(keys[2], (N_DP, pairs), BLK + 1, 2 * BLK + 1)
    large = jnp.where(hit, 2 * BLK, large)
    small = jax.random.randint(keys[3], (N_DP, pairs, 2), 1, BLK + 1)
    first = jnp.where(merged == 1, large, small[:, :, 0])
    second = jnp.where(merged == 1, 0, small[:, :, 1])
    return jnp.stack([first, second], axis=-1).reshape(N_DP, 2 * pairs).astype(jnp.int32)


def draw_upstream(key, part):
    key = jax.random.fold_in(key, 37)
    keys = jax.random.split(key, 1)
    along = jnp.arange(SEQ, dtype=jnp.float32) / (SEQ - 1)
    groups = jnp.arange(N_DP, dtype=jnp.float32) / max(N_DP - 1, 1)
    scale = (1.0 + 2.0 * along)[None, :, None] * (1.0 + 2.0 * groups)[:, None, None] / 3.0
    base = jnp.clip(jax.random.normal(keys[0], (N_DP, SEQ, HEADS * HDIM), jnp.float32), -6.0, 6.0)
    return (base * scale).astype(jnp.bfloat16)


def steps_of(rng, dims, shards, least, high):
    level = 1.0
    for axis_at, parts in shards:
        draws = jax.random.uniform(jax.random.fold_in(jax.random.fold_in(rng, 6), axis_at), (parts,), jnp.float32, least / len(shards), high / len(shards))
        level = level * jnp.repeat(jnp.exp(draws), dims[axis_at] // parts).reshape((-1,) + (1,) * (len(dims) - 1 - axis_at))
    return level


def bell_draw(own_key, extent, deviation, limit, pieces=(), kind=jnp.bfloat16):
    result = deviation * jax.random.normal(own_key, extent, jnp.float32)
    if pieces:
        result = result * steps_of(own_key, extent, pieces, -0.22, 0.18)
    return jnp.clip(result, -limit, limit).astype(kind)


def setup_inputs(seed: int = 0) -> dict:
    key_list = jax.random.split(jax.random.key(seed), 9)
    return {
        "patches": draw_patches(jax.random.fold_in(key_list[8], 71), 0),
        "counts": draw_counts(jax.random.fold_in(key_list[8], 71), 0),
        "norm_gain": jnp.clip(1.0 + 0.1 * jax.random.normal(key_list[2], (D,), jnp.float32), 0.5, 1.5),
        "norm_bias": bell_draw(key_list[3], (D,), 0.5, 3.0, (), jnp.float32),
        "qkv_weight": bell_draw(key_list[4], (D, 3, HEADS * HDIM), D ** -0.5, 0.109375, ((2, 16),)),
        "query_gain": jnp.clip(1.0 + 0.18 * jax.random.normal(key_list[5], (HEADS * HDIM,), jnp.float32), 0.1, 1.9),
        "key_gain": jnp.clip(1.0 + 0.18 * jax.random.normal(key_list[6], (HEADS * HDIM,), jnp.float32), 0.1, 1.9),
        "upstream": draw_upstream(jax.random.fold_in(key_list[8], 71), 0),
    }


EPS = 1e-06

def standardize(values):
    wide = values.astype(jnp.float32)
    centred = wide - lax.optimization_barrier(jnp.mean(wide, axis=-1, keepdims=True))
    factor = lax.rsqrt(lax.optimization_barrier(jnp.mean(centred * centred, axis=-1, keepdims=True)) + EPS)
    return (centred * factor, factor)

def norm_back(grad_out, hat, factor, gain):
    scaled = grad_out * gain
    return factor * (scaled - lax.optimization_barrier(jnp.mean(scaled, axis=-1, keepdims=True)) - hat * lax.optimization_barrier(jnp.mean(scaled * hat, axis=-1, keepdims=True)))

def image_labels(count_row, length):
    positions = jnp.arange(length, dtype=jnp.int32)
    block = positions // BLK
    first = block // 2 * 2
    slots = jnp.arange(count_row.shape[0], dtype=jnp.int32)
    first_count = lax.optimization_barrier(jnp.sum(jnp.where(first[:, None] == slots[None, :], count_row[None, :], 0), axis=1))
    image = jnp.where(first_count > BLK, first, block)
    image_count = lax.optimization_barrier(jnp.sum(jnp.where(image[:, None] == slots[None, :], count_row[None, :], 0), axis=1))
    offset = positions - image * BLK
    return jnp.where(offset < image_count, image, -1 - block).astype(jnp.int32)

def attend(q_scaled, k_scaled, values, d_out, labels):
    length, heads, size = q_scaled.shape
    blocks = length // ABLK

    def split(arr):
        return arr.reshape(blocks, ABLK, heads, size).astype(jnp.float32)
    q_blk, k_blk, v_blk, g_blk = (split(q_scaled), split(k_scaled), split(values), split(d_out))
    lab = labels.reshape(blocks, ABLK)
    mask = (lab[:, :, None] == lab[:, None, :])[:, None].astype(jnp.float32)
    scale = 1.0 / math.sqrt(size)
    scores = jnp.einsum('bqhd,bkhd->bhqk', q_blk, k_blk) * scale
    weights = jnp.exp(scores) * mask
    probs = weights / lax.optimization_barrier(jnp.sum(weights, axis=-1, keepdims=True))
    probs_b = probs.astype(jnp.bfloat16).astype(jnp.float32)
    output = jnp.einsum('bhqk,bkhd->bqhd', probs_b, v_blk).astype(jnp.bfloat16)
    dprob = jnp.einsum('bqhd,bkhd->bhqk', g_blk, v_blk)
    dvalue = jnp.einsum('bhqk,bqhd->bkhd', probs_b, g_blk)
    dscore = (probs * (dprob - lax.optimization_barrier(jnp.sum(probs * dprob, axis=-1, keepdims=True))) * scale).astype(jnp.bfloat16).astype(jnp.float32)
    dquery = jnp.einsum('bhqk,bkhd->bqhd', dscore, k_blk)
    dkey = jnp.einsum('bhqk,bqhd->bkhd', dscore, q_blk)
    shape = (length, heads, size)
    return (output.reshape(shape), dquery.reshape(shape), dkey.reshape(shape), dvalue.reshape(shape))

def reference(patches, counts, norm_gain, norm_bias, qkv_weight, query_gain, key_gain, upstream):
    length = patches.shape[1]
    width = patches.shape[2]
    total = qkv_weight.shape[2]
    heads = total // HDIM
    flat_weight = qkv_weight.reshape(width, 3 * total)
    q_gains = query_gain.reshape(heads, HDIM)
    k_gains = key_gain.reshape(heads, HDIM)

    def group(carry, inputs):
        rows_in, count_row, grad_rows = inputs
        hat, factor = standardize(rows_in)
        normed = (hat * norm_gain + norm_bias).astype(jnp.bfloat16)
        projected = jnp.dot(normed, flat_weight, preferred_element_type=jnp.float32).reshape(length, 3, heads, HDIM)
        q_hat, q_factor = standardize(projected[:, 0])
        k_hat, k_factor = standardize(projected[:, 1])
        q_scaled = (q_hat * q_gains).astype(jnp.bfloat16)
        k_scaled = (k_hat * k_gains).astype(jnp.bfloat16)
        values = projected[:, 2].astype(jnp.bfloat16)
        labels = image_labels(count_row, length)
        output, dquery, dkey, dvalue = attend(q_scaled, k_scaled, values, grad_rows.reshape(length, heads, HDIM), labels)
        q_term = lax.optimization_barrier(jnp.sum(dquery * q_hat, axis=0)).reshape(total)
        k_term = lax.optimization_barrier(jnp.sum(dkey * k_hat, axis=0)).reshape(total)
        dproj = jnp.stack([norm_back(dquery, q_hat, q_factor, q_gains), norm_back(dkey, k_hat, k_factor, k_gains), dvalue], axis=1)
        dproj = dproj.astype(jnp.bfloat16).reshape(length, 3 * total)
        w_term = jnp.dot(normed.T, dproj, preferred_element_type=jnp.float32)
        dnormed = jnp.dot(dproj, flat_weight.T, preferred_element_type=jnp.float32)
        gain_term = lax.optimization_barrier(jnp.sum(dnormed * hat, axis=0))
        bias_term = lax.optimization_barrier(jnp.sum(dnormed, axis=0))
        d_rows = norm_back(dnormed, hat, factor, norm_gain).astype(jnp.bfloat16)
        sums = (carry[0] + w_term, carry[1] + gain_term, carry[2] + bias_term, carry[3] + q_term, carry[4] + k_term)
        return (sums, (output.reshape(length, total), d_rows))
    start = (jnp.zeros((width, 3 * total), jnp.float32), jnp.zeros((width,), jnp.float32), jnp.zeros((width,), jnp.float32), jnp.zeros((total,), jnp.float32), jnp.zeros((total,), jnp.float32))
    sums, stacked = lax.scan(group, start, (patches, counts, upstream))
    factor = 1.0 / math.sqrt(N_DP * length)
    return (stacked[0], stacked[1], (sums[0] * factor).reshape(width, 3, total), sums[1] * factor, sums[2] * factor, sums[3] * factor, sums[4] * factor)
```

```python
import functools
import math

import jax
import jax.numpy as jnp
from jax import lax
from jax.experimental import pallas as pl
from jax.experimental.pallas import tpu as pltpu
from jax.sharding import PartitionSpec as P

HDIM = 128
BLK = 128
EPS = 1e-06
AXES = ("dp", "tensor")
N_DP = 8
N_T = 16
VMEM_LIMIT = 56 * 1024 * 1024
F32 = jnp.float32
BF16 = jnp.bfloat16


def ring_pairs(ring, flip):
    pairs = []
    for dp in range(N_DP):
        for t in range(N_T):
            along_x = (dp % 2 == 0) == (ring == 1)
            pairs.append((dp * N_T + t, dp * N_T + (t ^ (flip if along_x else 4 * flip))))
    return pairs


def swap(value, ring, flip):
    return lax.ppermute(value, AXES, ring_pairs(ring, flip))


def spread(value, ring):
    half = value.shape[0] // 2
    from1 = swap(value, ring, 1)
    from3 = swap(value, ring, 3)
    far_top = swap(from3[:half], ring, 1)
    far_bottom = swap(from1[half:], ring, 3)
    return from1, far_top, far_bottom, from3


def add(left, right):
    return (left.astype(F32) + right.astype(F32)).astype(BF16)


def fold(own, next1, far_top, far_bottom, next3, ring):
    half = far_top.shape[0]
    top = swap(far_top, ring, 3)
    bottom = swap(far_bottom, ring, 1)
    send1 = jnp.concatenate([add(next1[:half], top), next1[half:]], axis=0)
    send3 = jnp.concatenate([next3[:half], add(next3[half:], bottom)], axis=0)
    got1 = swap(send1, ring, 1)
    got3 = swap(send3, ring, 3)
    return own, got1, got3


def centre(wide):
    centred = wide - jnp.mean(wide, axis=-1, keepdims=True)
    factor = lax.rsqrt(jnp.mean(centred * centred, axis=-1, keepdims=True) + EPS)
    return centred * factor, factor


def norm_kernel(x_ref, gain_ref, bias_ref, out_ref):
    hat, _ = centre(x_ref[...].astype(F32))
    out_ref[...] = (hat * gain_ref[...] + bias_ref[...]).astype(BF16)


def norm_rows(x, gain, bias):
    rows, width = x.shape
    tile = 32
    return pl.pallas_call(
        norm_kernel,
        grid=(rows // tile,),
        in_specs=[
            pl.BlockSpec((tile, width), lambda i: (i, 0)),
            pl.BlockSpec((1, width), lambda i: (0, 0)),
            pl.BlockSpec((1, width), lambda i: (0, 0)),
        ],
        out_specs=pl.BlockSpec((tile, width), lambda i: (i, 0)),
        out_shape=jax.ShapeDtypeStruct((rows, width), BF16),
        name="norm_rows",
    )(x, gain, bias)


def patch_kernel(x_ref, gain_ref, own_ref, got1_ref, got3_ref, out_ref):
    hat, factor = centre(x_ref[...].astype(F32))
    grad = own_ref[...].astype(F32) + got1_ref[...].astype(F32) + got3_ref[...].astype(F32)
    scaled = grad * gain_ref[...]
    out_ref[...] = (
        factor
        * (
            scaled
            - jnp.mean(scaled, axis=-1, keepdims=True)
            - hat * jnp.mean(scaled * hat, axis=-1, keepdims=True)
        )
    ).astype(BF16)


def patch_rows(x, gain, own, got1, got3):
    rows, width = x.shape
    tile = 32
    block = pl.BlockSpec((tile, width), lambda i: (i, 0))
    return pl.pallas_call(
        patch_kernel,
        grid=(rows // tile,),
        in_specs=[block, pl.BlockSpec((1, width), lambda i: (0, 0)), block, block, block],
        out_specs=block,
        out_shape=jax.ShapeDtypeStruct((rows, width), BF16),
        name="patch_rows",
    )(x, gain, own, got1, got3)


def shard_labels(counts_ref, shard, shape, dim):
    first = (shard // 2) * 2
    merged = counts_ref[first] > BLK
    image = jnp.where(merged, first, shard)
    count = counts_ref[image]
    offset = lax.broadcasted_iota(jnp.int32, shape, dim) + BLK * (shard - image)
    return jnp.where(offset < count, image, -1 - shard)


def nt(left, right):
    return lax.dot_general(left, right, (((1,), (1,)), ((), ())), preferred_element_type=F32)


def tn(left, right):
    return lax.dot_general(left, right, (((0,), (0,)), ((), ())), preferred_element_type=F32)


def back(grad, hat, factor, gain):
    scaled = grad * gain
    return factor * (
        scaled
        - jnp.mean(scaled, axis=-1, keepdims=True)
        - hat * jnp.mean(scaled * hat, axis=-1, keepdims=True)
    )


def quad_kernel(n_top, n_bottom, first, meta, counts, *refs):
    refs = list(refs)
    tops = [refs.pop(0) for _ in range(n_top)]
    bottoms = [refs.pop(0) for _ in range(n_bottom)]
    w_ref, up_ref, qg_ref, kg_ref = [refs.pop(0) for _ in range(4)]
    if not first:
        refs.pop(0)
    att_ref = refs.pop(0)
    dn_tops = [refs.pop(0) for _ in range(n_top)]
    dn_bottoms = [refs.pop(0) for _ in range(n_bottom)]
    dproj_ref, terms_ref, proj, dbuf, abuf, sems = refs
    core = meta[0]
    places = [0, 1 + core, 2 - core, 3]

    def rows_of(place):
        return pl.ds(pl.multiple_of(place * BLK, BLK), BLK)

    def load(parts):
        return parts[0][...] if len(parts) == 1 else jnp.concatenate([p[...] for p in parts], axis=0)

    for side, parts in enumerate((tops, bottoms)):
        result = jnp.dot(load(parts), w_ref[...], preferred_element_type=F32)
        for k in range(2):
            proj[rows_of(places[2 * side + k]), :] = result[k * BLK : (k + 1) * BLK]

    scale = 1.0 / math.sqrt(HDIM)
    q_terms = [None, None]
    k_terms = [None, None]
    copies = []
    for pair in range(2):
        shards = [meta[1 + 2 * pair + k] for k in range(2)]
        columns = jnp.concatenate([shard_labels(counts, s, (BLK, 1), 0) for s in shards], axis=0)
        across = jnp.concatenate([shard_labels(counts, s, (1, BLK), 1) for s in shards], axis=1)
        same = columns == across
        rows = slice(pair * 2 * BLK, (pair + 1) * 2 * BLK)
        for head in range(2):
            cols = slice(head * HDIM, (head + 1) * HDIM)
            q_gain = qg_ref[:, cols]
            k_gain = kg_ref[:, cols]
            q_hat, q_factor = centre(proj[rows, head * HDIM : (head + 1) * HDIM])
            k_hat, k_factor = centre(proj[rows, (2 + head) * HDIM : (3 + head) * HDIM])
            value = proj[rows, (4 + head) * HDIM : (5 + head) * HDIM].astype(BF16)
            q_s = (q_hat * q_gain).astype(BF16)
            k_s = (k_hat * k_gain).astype(BF16)
            grad = jnp.concatenate([up_ref[rows_of(s), cols] for s in shards], axis=0)
            weights = jnp.where(same, jnp.exp(nt(q_s, k_s) * scale), 0.0)
            probs = weights * (1.0 / jnp.sum(weights, axis=-1, keepdims=True))
            probs_b = probs.astype(BF16)
            abuf[rows, cols] = jnp.dot(probs_b, value, preferred_element_type=F32).astype(BF16)
            dprob = nt(grad, value)
            inner = jnp.sum(probs * dprob, axis=-1, keepdims=True)
            dscore = (probs * (dprob - inner) * scale).astype(BF16)
            dvalue = tn(probs_b, grad)
            dquery = jnp.dot(dscore, k_s, preferred_element_type=F32)
            dkey = tn(dscore, q_s)
            q_term = jnp.sum(dquery * q_hat, axis=0, keepdims=True)
            k_term = jnp.sum(dkey * k_hat, axis=0, keepdims=True)
            q_terms[head] = q_term if pair == 0 else q_terms[head] + q_term
            k_terms[head] = k_term if pair == 0 else k_terms[head] + k_term
            dbuf[rows, head * HDIM : (head + 1) * HDIM] = back(dquery, q_hat, q_factor, q_gain).astype(BF16)
            dbuf[rows, (2 + head) * HDIM : (3 + head) * HDIM] = back(dkey, k_hat, k_factor, k_gain).astype(BF16)
            dbuf[rows, (4 + head) * HDIM : (5 + head) * HDIM] = dvalue.astype(BF16)
        for k in range(2):
            place = 2 * pair + k
            copy = pltpu.make_async_copy(
                abuf.at[pl.ds(place * BLK, BLK)], att_ref.at[rows_of(shards[k])], sems.at[place]
            )
            copy.start()
            copies.append(copy)
    terms_ref[...] = jnp.concatenate(q_terms + k_terms, axis=1)

    for side, outs in enumerate((dn_tops, dn_bottoms)):
        part = jnp.concatenate([dbuf[rows_of(places[2 * side + k]), :] for k in range(2)], axis=0)
        dproj_ref[side * 2 * BLK : (side + 1) * 2 * BLK] = part
        result = nt(part, w_ref[...]).astype(BF16)
        start = 0
        for out in outs:
            out[...] = result[start : start + out.shape[0]]
            start += out.shape[0]
    for copy in copies:
        copy.wait()


def quad(meta, counts, tops, bottoms, weight, upstream, q_gain, k_gain, attention):
    width, cols = weight.shape
    length, heads = upstream.shape
    first = attention is None
    vmem = pl.BlockSpec(memory_space=pltpu.VMEM)
    smem = pl.BlockSpec(memory_space=pltpu.SMEM)
    anywhere = pl.BlockSpec(memory_space=pl.ANY)
    operands = [meta, counts, *tops, *bottoms, weight, upstream, q_gain, k_gain]
    in_specs = [smem, smem] + [vmem] * (len(operands) - 2)
    aliases = {}
    if not first:
        aliases = {len(operands): 0}
        operands.append(attention)
        in_specs.append(anywhere)
    parts = [*tops, *bottoms]
    outs = pl.pallas_call(
        functools.partial(quad_kernel, len(tops), len(bottoms), first),
        in_specs=in_specs,
        out_specs=[anywhere] + [vmem] * (len(parts) + 2),
        out_shape=[jax.ShapeDtypeStruct((length, heads), BF16)]
        + [jax.ShapeDtypeStruct(p.shape, BF16) for p in parts]
        + [jax.ShapeDtypeStruct((4 * BLK, cols), BF16), jax.ShapeDtypeStruct((1, 2 * heads), F32)],
        scratch_shapes=[
            pltpu.VMEM((4 * BLK, cols), F32),
            pltpu.VMEM((4 * BLK, cols), BF16),
            pltpu.VMEM((4 * BLK, heads), BF16),
            pltpu.SemaphoreType.DMA((4,)),
        ],
        input_output_aliases=aliases,
        compiler_params=pltpu.CompilerParams(vmem_limit_bytes=VMEM_LIMIT),
        cost_estimate=pl.CostEstimate(
            flops=4 * 4 * BLK * width * cols + 12 * 4 * BLK * 2 * BLK * heads,
            bytes_accessed=2 * width * cols + 4 * 4 * BLK * width,
            transcendentals=8 * BLK * 2 * BLK * 2,
        ),
        name="quad",
    )(*operands)
    attention = outs[0]
    top_outs = outs[1 : 1 + len(tops)]
    bottom_outs = outs[1 + len(tops) : 1 + len(parts)]
    return attention, list(top_outs), list(bottom_outs), outs[-2], outs[-1]


def weight_kernel(n_rows, *refs):
    rows = refs[:n_rows]
    dprojs = refs[n_rows : n_rows + 4]
    w_ref, gain_ref, bias_ref, out_ref, gain_out, shift_out, column_sum = refs[n_rows + 4 :]

    @pl.when(pl.program_id(0) == 0)
    def _():
        total = jnp.sum(dprojs[0][...].astype(F32), axis=0, keepdims=True)
        for ref in dprojs[1:]:
            total = total + jnp.sum(ref[...].astype(F32), axis=0, keepdims=True)
        column_sum[...] = total

    left = jnp.concatenate([ref[...] for ref in rows], axis=0)
    right = jnp.concatenate([ref[...] for ref in dprojs], axis=0)
    grad = tn(left, right)
    out_ref[...] = grad.astype(BF16)
    weight = w_ref[...].astype(F32)

    def over_columns(value):
        lanes = value[:, :HDIM]
        for start in range(HDIM, value.shape[1], HDIM):
            lanes = lanes + value[:, start : start + HDIM]
        return jnp.sum(lanes.T, axis=0, keepdims=True)

    shift = over_columns(weight * column_sum[...])
    shift_out[...] = shift
    gain_out[...] = (over_columns(weight * grad) - bias_ref[...] * shift) / gain_ref[...]


def weight_grads(rows, dprojs, weight, gain, bias):
    width, cols = weight.shape
    tile = 256
    wide = pl.BlockSpec((1, tile), lambda i: (0, i))
    return pl.pallas_call(
        functools.partial(weight_kernel, len(rows)),
        grid=(width // tile,),
        in_specs=[pl.BlockSpec((r.shape[0], tile), lambda i: (0, i)) for r in rows]
        + [pl.BlockSpec(d.shape, lambda i: (0, 0)) for d in dprojs]
        + [pl.BlockSpec((tile, cols), lambda i: (i, 0)), wide, wide],
        out_specs=[pl.BlockSpec((tile, cols), lambda i: (i, 0)), wide, wide],
        out_shape=[
            jax.ShapeDtypeStruct((width, cols), BF16),
            jax.ShapeDtypeStruct((1, width), F32),
            jax.ShapeDtypeStruct((1, width), F32),
        ],
        scratch_shapes=[pltpu.VMEM((1, cols), F32)],
        compiler_params=pltpu.CompilerParams(vmem_limit_bytes=VMEM_LIMIT),
        cost_estimate=pl.CostEstimate(
            flops=2 * 16 * BLK * width * cols,
            bytes_accessed=4 * width * cols + 2 * 16 * BLK * (width + cols),
            transcendentals=0,
        ),
        name="weight_grads",
    )(*rows, *dprojs, weight, gain, bias)


def quad_meta(core, tensor, i, j):
    found = [core]
    for place in range(4):
        straight = (i + place // 2) * 4 + j + place % 2
        turned = (j + place // 2) * 4 + i + place % 2
        found.append(tensor ^ jnp.where(core == 0, straight, turned))
    return jnp.stack(found).astype(jnp.int32)


def total_over(value, axis, flips):
    size = lax.axis_size(axis)
    for flip in flips:
        value = value + lax.ppermute(value, axis, [(k, k ^ flip) for k in range(size)])
    return value


def body(patches, counts, norm_gain, norm_bias, qkv_weight, query_gain, key_gain, upstream):
    width = patches.shape[2]
    local = qkv_weight.shape[2]
    length = upstream.shape[1]
    core = lax.axis_index("dp") % 2
    tensor = lax.axis_index("tensor")
    weight = qkv_weight.reshape(width, 3 * local)
    gain = norm_gain.reshape(1, width)
    bias = norm_bias.reshape(1, width)
    own_rows = patches[0]

    own = norm_rows(own_rows, gain, bias)
    near, top, bottom, next3 = spread(own, 1)
    groups = []
    for group in (jnp.concatenate([own, near], axis=0), jnp.concatenate([top, bottom, next3], axis=0)):
        from1, far_top, far_bottom, from3 = spread(group, 2)
        groups.append((group, from1, far_top, far_bottom, from3))

    attention = None
    dprojs = []
    rows = []
    terms = None
    halves = {}
    for i, g in ((0, 0), (2, 0), (0, 1), (2, 1)):
        parts = groups[g]
        tops, bottoms = ([parts[0]], [parts[1]]) if i == 0 else ([parts[2], parts[3]], [parts[4]])
        attention, dn_top, dn_bottom, dproj, term = quad(
            quad_meta(core, tensor, i, 2 * g),
            counts[0],
            tops,
            bottoms,
            weight,
            upstream[0],
            query_gain.reshape(1, local),
            key_gain.reshape(1, local),
            attention,
        )
        halves[i, g] = dn_top + dn_bottom
        rows += tops + bottoms
        dprojs.append(dproj)
        terms = term if terms is None else terms + term

    sums = []
    for g in (0, 1):
        slot0, slot1 = halves[0, g]
        far_top, far_bottom, slot3 = halves[2, g]
        parts = fold(slot0, slot1, far_top, far_bottom, slot3, 2)
        sums.append(sum(p.astype(F32) for p in parts).astype(BF16))
    half = BLK // 2
    pieces = fold(
        sums[0][:BLK],
        sums[0][BLK:],
        sums[1][:half],
        sums[1][half:BLK],
        sums[1][BLK:],
        1,
    )
    patch_grad = patch_rows(own_rows, gain, *pieces)

    weight_part, gain_part, shift_part = weight_grads(rows, dprojs, weight, gain, bias)
    factor = 1.0 / math.sqrt(lax.axis_size("dp") * length)
    weight_share = lax.psum_scatter(weight_part, "dp", scatter_dimension=0, tiled=True).astype(F32)
    weight_grad = (weight_share * factor).reshape(weight_share.shape[0], 3, local)
    norms = total_over(jnp.concatenate([gain_part, shift_part], axis=1), "tensor", (1, 2, 4, 8))
    small = total_over(jnp.concatenate([norms, terms], axis=1), "dp", (1, 2, 4))[0] * factor
    return (
        attention.reshape(1, length, local),
        patch_grad[None],
        weight_grad,
        small[:width],
        small[width : 2 * width],
        small[2 * width : 2 * width + local],
        small[2 * width + local :],
    )


def solution(mesh):
    in_specs = (
        P("dp", "tensor", None),
        P("dp", None),
        P(),
        P(),
        P(None, None, "tensor"),
        P("tensor"),
        P("tensor"),
        P("dp", None, "tensor"),
    )
    out_specs = (
        P("dp", None, "tensor"),
        P("dp", "tensor", None),
        P("dp", None, "tensor"),
        P(),
        P(),
        P("tensor"),
        P("tensor"),
    )
    return jax.shard_map(body, mesh=mesh, in_specs=in_specs, out_specs=out_specs, check_vma=False)
```

```python
import functools
import math

import jax
import jax.numpy as jnp
from jax import lax
from jax.experimental import pallas as pl
from jax.experimental.pallas import tpu as pltpu
from jax.sharding import PartitionSpec as P

HDIM = 128
BLK = 128
EPS = 1e-06
AXES = ("dp", "tensor")
N_DP = 8
N_T = 16
VMEM_LIMIT = 26 * 1024 * 1024
F32 = jnp.float32
BF16 = jnp.bfloat16


def ring_pairs(ring, flip):
    pairs = []
    for dp in range(N_DP):
        for t in range(N_T):
            along_x = (dp % 2 == 0) == (ring == 1)
            pairs.append((dp * N_T + t, dp * N_T + (t ^ (flip if along_x else 4 * flip))))
    return pairs


def swap(value, ring, flip):
    return lax.ppermute(value, AXES, ring_pairs(ring, flip))


def spread(value, ring):
    half = value.shape[0] // 2
    from1 = swap(value, ring, 1)
    from3 = swap(value, ring, 3)
    far_top = swap(from3[:half], ring, 1)
    far_bottom = swap(from1[half:], ring, 3)
    return from1, far_top, far_bottom, from3


def add(left, right):
    return (left.astype(F32) + right.astype(F32)).astype(BF16)


def fold(own, next1, far_top, far_bottom, next3, ring):
    half = far_top.shape[0]
    top = swap(far_top, ring, 3)
    bottom = swap(far_bottom, ring, 1)
    send1 = jnp.concatenate([add(next1[:half], top), next1[half:]], axis=0)
    send3 = jnp.concatenate([next3[:half], add(next3[half:], bottom)], axis=0)
    got1 = swap(send1, ring, 1)
    got3 = swap(send3, ring, 3)
    return own, got1, got3


def centre(wide):
    centred = wide - jnp.mean(wide, axis=-1, keepdims=True)
    factor = lax.rsqrt(jnp.mean(centred * centred, axis=-1, keepdims=True) + EPS)
    return centred * factor, factor


def norm_kernel(x_ref, gain_ref, bias_ref, out_ref):
    hat, _ = centre(x_ref[...].astype(F32))
    out_ref[...] = (hat * gain_ref[...] + bias_ref[...]).astype(BF16)


def norm_rows(x, gain, bias):
    rows, width = x.shape
    tile = 32
    return pl.pallas_call(
        norm_kernel,
        grid=(rows // tile,),
        in_specs=[
            pl.BlockSpec((tile, width), lambda i: (i, 0)),
            pl.BlockSpec((1, width), lambda i: (0, 0)),
            pl.BlockSpec((1, width), lambda i: (0, 0)),
        ],
        out_specs=pl.BlockSpec((tile, width), lambda i: (i, 0)),
        out_shape=jax.ShapeDtypeStruct((rows, width), BF16),
        name="norm_rows",
    )(x, gain, bias)


def patch_kernel(x_ref, gain_ref, own_ref, got1_ref, got3_ref, out_ref):
    hat, factor = centre(x_ref[...].astype(F32))
    grad = own_ref[...].astype(F32) + got1_ref[...].astype(F32) + got3_ref[...].astype(F32)
    scaled = grad * gain_ref[...]
    out_ref[...] = (
        factor
        * (
            scaled
            - jnp.mean(scaled, axis=-1, keepdims=True)
            - hat * jnp.mean(scaled * hat, axis=-1, keepdims=True)
        )
    ).astype(BF16)


def patch_rows(x, gain, own, got1, got3):
    rows, width = x.shape
    tile = 32
    block = pl.BlockSpec((tile, width), lambda i: (i, 0))
    return pl.pallas_call(
        patch_kernel,
        grid=(rows // tile,),
        in_specs=[block, pl.BlockSpec((1, width), lambda i: (0, 0)), block, block, block],
        out_specs=block,
        out_shape=jax.ShapeDtypeStruct((rows, width), BF16),
        name="patch_rows",
    )(x, gain, own, got1, got3)


def shard_labels(counts_ref, shard, shape, dim):
    first = (shard // 2) * 2
    merged = counts_ref[first] > BLK
    image = jnp.where(merged, first, shard)
    count = counts_ref[image]
    offset = lax.broadcasted_iota(jnp.int32, shape, dim) + BLK * (shard - image)
    return jnp.where(offset < count, image, -1 - shard)


def whole(w_ref):
    return jnp.concatenate([w_ref[part] for part in range(3)], axis=1)


def nt(left, right):
    return lax.dot_general(left, right, (((1,), (1,)), ((), ())), preferred_element_type=F32)


def tn(left, right):
    return lax.dot_general(left, right, (((0,), (0,)), ((), ())), preferred_element_type=F32)


def back(grad, hat, factor, gain):
    scaled = grad * gain
    return factor * (
        scaled
        - jnp.mean(scaled, axis=-1, keepdims=True)
        - hat * jnp.mean(scaled * hat, axis=-1, keepdims=True)
    )


def quad_kernel(n_top, n_bottom, first, meta, counts, *refs):
    refs = list(refs)
    tops = [refs.pop(0) for _ in range(n_top)]
    bottoms = [refs.pop(0) for _ in range(n_bottom)]
    w_ref, up_ref, qg_ref, kg_ref = [refs.pop(0) for _ in range(4)]
    if not first:
        refs.pop(0)
    att_ref = refs.pop(0)
    dn_tops = [refs.pop(0) for _ in range(n_top)]
    dn_bottoms = [refs.pop(0) for _ in range(n_bottom)]
    dproj_ref, terms_ref, proj, dbuf, abuf, sems = refs
    core = meta[0]
    places = [0, 1 + core, 2 - core, 3]

    def rows_of(place):
        return pl.ds(pl.multiple_of(place * BLK, BLK), BLK)

    def load(parts):
        return parts[0][...] if len(parts) == 1 else jnp.concatenate([p[...] for p in parts], axis=0)

    for side, parts in enumerate((tops, bottoms)):
        result = jnp.dot(load(parts), whole(w_ref), preferred_element_type=F32)
        for k in range(2):
            proj[rows_of(places[2 * side + k]), :] = result[k * BLK : (k + 1) * BLK]

    scale = 1.0 / math.sqrt(HDIM)
    q_terms = [None, None]
    k_terms = [None, None]
    copies = []
    for pair in range(2):
        shards = [meta[1 + 2 * pair + k] for k in range(2)]
        columns = jnp.concatenate([shard_labels(counts, s, (BLK, 1), 0) for s in shards], axis=0)
        across = jnp.concatenate([shard_labels(counts, s, (1, BLK), 1) for s in shards], axis=1)
        same = columns == across
        rows = slice(pair * 2 * BLK, (pair + 1) * 2 * BLK)
        for head in range(2):
            cols = slice(head * HDIM, (head + 1) * HDIM)
            q_gain = qg_ref[:, cols]
            k_gain = kg_ref[:, cols]
            q_hat, q_factor = centre(proj[rows, head * HDIM : (head + 1) * HDIM])
            k_hat, k_factor = centre(proj[rows, (2 + head) * HDIM : (3 + head) * HDIM])
            value = proj[rows, (4 + head) * HDIM : (5 + head) * HDIM].astype(BF16)
            q_s = (q_hat * q_gain).astype(BF16)
            k_s = (k_hat * k_gain).astype(BF16)
            grad = jnp.concatenate([up_ref[rows_of(s), cols] for s in shards], axis=0)
            weights = jnp.where(same, jnp.exp(nt(q_s, k_s) * scale), 0.0)
            probs = weights * (1.0 / jnp.sum(weights, axis=-1, keepdims=True))
            probs_b = probs.astype(BF16)
            abuf[rows, cols] = jnp.dot(probs_b, value, preferred_element_type=F32).astype(BF16)
            dprob = nt(grad, value)
            inner = jnp.sum(probs * dprob, axis=-1, keepdims=True)
            dscore = (probs * (dprob - inner) * scale).astype(BF16)
            dvalue = tn(probs_b, grad)
            dquery = jnp.dot(dscore, k_s, preferred_element_type=F32)
            dkey = tn(dscore, q_s)
            q_term = jnp.sum(dquery * q_hat, axis=0, keepdims=True)
            k_term = jnp.sum(dkey * k_hat, axis=0, keepdims=True)
            q_terms[head] = q_term if pair == 0 else q_terms[head] + q_term
            k_terms[head] = k_term if pair == 0 else k_terms[head] + k_term
            dbuf[rows, head * HDIM : (head + 1) * HDIM] = back(dquery, q_hat, q_factor, q_gain).astype(BF16)
            dbuf[rows, (2 + head) * HDIM : (3 + head) * HDIM] = back(dkey, k_hat, k_factor, k_gain).astype(BF16)
            dbuf[rows, (4 + head) * HDIM : (5 + head) * HDIM] = dvalue.astype(BF16)
        for k in range(2):
            place = 2 * pair + k
            copy = pltpu.make_async_copy(
                abuf.at[pl.ds(place * BLK, BLK)], att_ref.at[rows_of(shards[k])], sems.at[place]
            )
            copy.start()
            copies.append(copy)
    terms_ref[...] = jnp.concatenate(q_terms + k_terms, axis=1)

    for side, outs in enumerate((dn_tops, dn_bottoms)):
        part = jnp.concatenate([dbuf[rows_of(places[2 * side + k]), :] for k in range(2)], axis=0)
        dproj_ref[side * 2 * BLK : (side + 1) * 2 * BLK] = part
        result = nt(part, whole(w_ref)).astype(BF16)
        start = 0
        for out in outs:
            out[...] = result[start : start + out.shape[0]]
            start += out.shape[0]
    for copy in copies:
        copy.wait()


def quad(meta, counts, tops, bottoms, weight, upstream, q_gain, k_gain, attention):
    width = weight.shape[1]
    length, heads = upstream.shape
    cols = 3 * heads
    first = attention is None
    vmem = pl.BlockSpec(memory_space=pltpu.VMEM)
    smem = pl.BlockSpec(memory_space=pltpu.SMEM)
    anywhere = pl.BlockSpec(memory_space=pl.ANY)
    operands = [meta, counts, *tops, *bottoms, weight, upstream, q_gain, k_gain]
    in_specs = [smem, smem] + [vmem] * (len(operands) - 2)
    aliases = {}
    if not first:
        aliases = {len(operands): 0}
        operands.append(attention)
        in_specs.append(anywhere)
    parts = [*tops, *bottoms]
    outs = pl.pallas_call(
        functools.partial(quad_kernel, len(tops), len(bottoms), first),
        in_specs=in_specs,
        out_specs=[anywhere] + [vmem] * (len(parts) + 2),
        out_shape=[jax.ShapeDtypeStruct((length, heads), BF16)]
        + [jax.ShapeDtypeStruct(p.shape, BF16) for p in parts]
        + [jax.ShapeDtypeStruct((4 * BLK, cols), BF16), jax.ShapeDtypeStruct((1, 2 * heads), F32)],
        scratch_shapes=[
            pltpu.VMEM((4 * BLK, cols), F32),
            pltpu.VMEM((4 * BLK, cols), BF16),
            pltpu.VMEM((4 * BLK, heads), BF16),
            pltpu.SemaphoreType.DMA((4,)),
        ],
        input_output_aliases=aliases,
        compiler_params=pltpu.CompilerParams(vmem_limit_bytes=VMEM_LIMIT),
        cost_estimate=pl.CostEstimate(
            flops=4 * 4 * BLK * width * cols + 12 * 4 * BLK * 2 * BLK * heads,
            bytes_accessed=2 * width * cols + 4 * 4 * BLK * width,
            transcendentals=8 * BLK * 2 * BLK * 2,
        ),
        name="quad",
    )(*operands)
    attention = outs[0]
    top_outs = outs[1 : 1 + len(tops)]
    bottom_outs = outs[1 + len(tops) : 1 + len(parts)]
    return attention, list(top_outs), list(bottom_outs), outs[-2], outs[-1]


def weight_kernel(n_rows, *refs):
    rows = refs[:n_rows]
    dprojs = refs[n_rows : n_rows + 4]
    w_ref, gain_ref, bias_ref = refs[n_rows + 4 : n_rows + 7]
    out_ref, gain_out, shift_out, column_sum = refs[-4:]

    @pl.when(pl.program_id(0) == 0)
    def _():
        total = jnp.sum(dprojs[0][...].astype(F32), axis=0, keepdims=True)
        for ref in dprojs[1:]:
            total = total + jnp.sum(ref[...].astype(F32), axis=0, keepdims=True)
        column_sum[...] = total

    left = jnp.concatenate([ref[...] for ref in rows], axis=0)
    right = jnp.concatenate([ref[...] for ref in dprojs], axis=0)
    grad = tn(left, right)
    out_ref[...] = grad.astype(BF16)
    weight = whole(w_ref).astype(F32)

    def over_columns(value):
        lanes = value[:, :HDIM]
        for start in range(HDIM, value.shape[1], HDIM):
            lanes = lanes + value[:, start : start + HDIM]
        return jnp.sum(lanes.T, axis=0, keepdims=True)

    shift = over_columns(weight * column_sum[...])
    shift_out[...] = shift
    gain_out[...] = (over_columns(weight * grad) - bias_ref[...] * shift) / gain_ref[...]


def weight_grads(rows, dprojs, weight, gain, bias, half, before):
    width = weight.shape[1]
    cols = 3 * weight.shape[2]
    tile = 256
    steps = width // tile // 2
    skip = half * steps
    wide = pl.BlockSpec((1, tile), lambda i: (0, i + skip))
    wide_out = pl.BlockSpec((1, tile), lambda i: (0, i))
    operands = [*rows, *dprojs, weight, gain, bias]
    more_specs = []
    aliases = {}
    if before is not None:
        aliases = {len(operands): 0}
        operands.append(before)
        more_specs = [pl.BlockSpec(memory_space=pl.ANY)]
    return pl.pallas_call(
        functools.partial(weight_kernel, len(rows)),
        grid=(steps,),
        in_specs=[pl.BlockSpec((r.shape[0], tile), lambda i: (0, i + skip)) for r in rows]
        + [pl.BlockSpec(d.shape, lambda i: (0, 0)) for d in dprojs]
        + [pl.BlockSpec((3, tile, cols // 3), lambda i: (0, i + skip, 0)), wide, wide]
        + more_specs,
        out_specs=[pl.BlockSpec((tile, cols), lambda i: (i + skip, 0)), wide_out, wide_out],
        out_shape=[
            jax.ShapeDtypeStruct((width, cols), BF16),
            jax.ShapeDtypeStruct((1, width // 2), F32),
            jax.ShapeDtypeStruct((1, width // 2), F32),
        ],
        input_output_aliases=aliases,
        scratch_shapes=[pltpu.VMEM((1, cols), F32)],
        compiler_params=pltpu.CompilerParams(vmem_limit_bytes=VMEM_LIMIT),
        cost_estimate=pl.CostEstimate(
            flops=16 * BLK * width * cols,
            bytes_accessed=2 * width * cols + 16 * BLK * (width + 2 * cols),
            transcendentals=0,
        ),
        name="weight_grads",
    )(*operands)


def share_kernel(factor, share_ref, out_ref):
    cols = out_ref.shape[2]
    for part in range(3):
        out_ref[part] = share_ref[:, part * cols : (part + 1) * cols].astype(F32) * factor


def weight_out(share, factor):
    rows, cols = share.shape
    tile = 128
    return pl.pallas_call(
        functools.partial(share_kernel, factor),
        grid=(rows // tile,),
        in_specs=[pl.BlockSpec((tile, cols), lambda i: (i, 0))],
        out_specs=pl.BlockSpec((3, tile, cols // 3), lambda i: (0, i, 0)),
        out_shape=jax.ShapeDtypeStruct((3, rows, cols // 3), F32),
        name="weight_out",
    )(share).transpose(1, 0, 2)


def quad_meta(core, tensor, i, j):
    found = [core]
    for place in range(4):
        straight = (i + place // 2) * 4 + j + place % 2
        turned = (j + place // 2) * 4 + i + place % 2
        found.append(tensor ^ jnp.where(core == 0, straight, turned))
    return jnp.stack(found).astype(jnp.int32)


def total_over(value, axis, flips):
    size = lax.axis_size(axis)
    for flip in flips:
        value = value + lax.ppermute(value, axis, [(k, k ^ flip) for k in range(size)])
    return value


def together(*values):
    return lax.optimization_barrier(values)


def body(patches, counts, norm_gain, norm_bias, qkv_weight, query_gain, key_gain, upstream):
    width = patches.shape[2]
    local = qkv_weight.shape[2]
    length = upstream.shape[1]
    factor = 1.0 / math.sqrt(lax.axis_size("dp") * length)
    core = lax.axis_index("dp") % 2
    tensor = lax.axis_index("tensor")
    gain = norm_gain.reshape(1, width)
    bias = norm_bias.reshape(1, width)
    own_rows = patches[0]
    half = BLK // 2

    own = norm_rows(own_rows, gain, bias)
    near, next3 = swap(own, 1, 1), swap(own, 1, 3)
    weight = qkv_weight.transpose(1, 0, 2)
    metas = [quad_meta(core, tensor, i, j) for i, j in ((0, 0), (2, 0), (0, 2), (2, 2))]
    near, next3, *metas = together(near, next3, *metas)
    top, bottom = swap(next3[:half], 1, 1), swap(near[half:], 1, 3)
    group0 = jnp.concatenate([own, near], axis=0)
    g0_1, g0_3 = swap(group0, 2, 1), swap(group0, 2, 3)
    group1 = jnp.concatenate([top, bottom, next3], axis=0)
    g1_1, g1_3 = swap(group1, 2, 1), swap(group1, 2, 3)
    g0_top, g0_bottom = swap(g0_3[:BLK], 2, 1), swap(g0_1[BLK:], 2, 3)
    g1_top, g1_bottom = swap(g1_3[:BLK], 2, 1), swap(g1_1[BLK:], 2, 3)

    def run(meta, tops, bottoms, attention):
        return quad(
            meta,
            counts[0],
            tops,
            bottoms,
            weight,
            upstream[0],
            query_gain.reshape(1, local),
            key_gain.reshape(1, local),
            attention,
        )

    attention, (r0_0,), (r0_1,), dproj0, terms0 = run(metas[0], [group0], [g0_1], None)
    attention, (f0_top, f0_bottom), (r0_3,), dproj1, terms1 = run(
        metas[1], [g0_top, g0_bottom], [g0_3], attention
    )
    n0_top, n0_bottom = swap(f0_top, 2, 3), swap(f0_bottom, 2, 1)
    attention, (r1_0,), (r1_1,), dproj2, terms2 = run(metas[2], [group1], [g1_1], attention)
    attention, g1_top, g1_bottom, n0_top, n0_bottom = together(
        attention, g1_top, g1_bottom, n0_top, n0_bottom
    )
    s0_1 = jnp.concatenate([add(r0_1[:BLK], n0_top), r0_1[BLK:]], axis=0)
    s0_3 = jnp.concatenate([r0_3[:BLK], add(r0_3[BLK:], n0_bottom)], axis=0)
    g1_top, s0_1, s0_3 = together(g1_top, s0_1, s0_3)
    t0_1, t0_3 = swap(s0_1, 2, 1), swap(s0_3, 2, 3)
    attention, (f1_top, f1_bottom), (r1_3,), dproj3, terms3 = run(
        metas[3], [g1_top, g1_bottom], [g1_3], attention
    )
    n1_top, n1_bottom = swap(f1_top, 2, 3), swap(f1_bottom, 2, 1)

    rows = [group0, g0_1, g0_top, g0_bottom, g0_3, group1, g1_1, g1_top, g1_bottom, g1_3]
    dprojs = [dproj0, dproj1, dproj2, dproj3]
    part, gain_a, shift_a = weight_grads(rows, dprojs, weight, gain, bias, 0, None)
    part, n1_top, n1_bottom, t0_1, t0_3 = together(part, n1_top, n1_bottom, t0_1, t0_3)
    s1_1 = jnp.concatenate([add(r1_1[:BLK], n1_top), r1_1[BLK:]], axis=0)
    s1_3 = jnp.concatenate([r1_3[:BLK], add(r1_3[BLK:], n1_bottom)], axis=0)
    part, s1_1, s1_3 = together(part, s1_1, s1_3)
    t1_1, t1_3 = swap(s1_1, 2, 1), swap(s1_3, 2, 3)
    part, gain_b, shift_b = weight_grads(rows, dprojs, weight, gain, bias, 1, part)
    share = lax.psum_scatter(part, "dp", scatter_dimension=0, tiled=True)
    sum0 = (r0_0.astype(F32) + t0_1.astype(F32) + t0_3.astype(F32)).astype(BF16)

    norms = jnp.concatenate([gain_a, gain_b, shift_a, shift_b], axis=1)
    norms = total_over(norms, "tensor", (1, 2, 4, 8))
    t1_1, t1_3, norms = together(t1_1, t1_3, norms)
    sum1 = (r1_0.astype(F32) + t1_1.astype(F32) + t1_3.astype(F32)).astype(BF16)

    u_top, u_bottom = swap(sum1[:half], 1, 3), swap(sum1[half:BLK], 1, 1)
    small = jnp.concatenate([norms, terms0 + terms1 + terms2 + terms3], axis=1)
    small = total_over(small, "dp", (1,))
    u_top, u_bottom, small = together(u_top, u_bottom, small)
    v1 = jnp.concatenate([add(sum0[BLK : BLK + half], u_top), sum0[BLK + half :]], axis=0)
    v3 = jnp.concatenate([sum1[BLK : BLK + half], add(sum1[BLK + half :], u_bottom)], axis=0)
    got1, got3 = swap(v1, 1, 1), swap(v3, 1, 3)
    small = total_over(small, "dp", (2, 4))[0] * factor
    got1, got3, small = together(got1, got3, small)
    patch_grad = patch_rows(own_rows, gain, sum0[:BLK], got1, got3)
    weight_grad = weight_out(share, factor)
    return (
        attention.reshape(1, length, local),
        patch_grad[None],
        weight_grad,
        small[:width],
        small[width : 2 * width],
        small[2 * width : 2 * width + local],
        small[2 * width + local :],
    )


def solution(mesh):
    in_specs = (
        P("dp", "tensor", None),
        P("dp", None),
        P(),
        P(),
        P(None, None, "tensor"),
        P("tensor"),
        P("tensor"),
        P("dp", None, "tensor"),
    )
    out_specs = (
        P("dp", None, "tensor"),
        P("dp", "tensor", None),
        P("dp", None, "tensor"),
        P(),
        P(),
        P("tensor"),
        P("tensor"),
    )
    return jax.shard_map(body, mesh=mesh, in_specs=in_specs, out_specs=out_specs, check_vma=False)
```

```python
import functools
import math

import jax
import jax.numpy as jnp
from jax import lax
from jax.experimental import pallas as pl
from jax.experimental.pallas import tpu as pltpu
from jax.sharding import PartitionSpec as P

HDIM = 128
BLK = 128
EPS = 1e-06
AXES = ("dp", "tensor")
N_DP = 8
N_T = 16
VMEM_LIMIT = 26 * 1024 * 1024
TINY = pl.CostEstimate(flops=1000, bytes_accessed=1000, transcendentals=0)
F32 = jnp.float32
BF16 = jnp.bfloat16


def ring_pairs(ring, flip):
    pairs = []
    for dp in range(N_DP):
        for t in range(N_T):
            along_x = (dp % 2 == 0) == (ring == 1)
            pairs.append((dp * N_T + t, dp * N_T + (t ^ (flip if along_x else 4 * flip))))
    return pairs


def swap(value, ring, flip):
    return lax.ppermute(value, AXES, ring_pairs(ring, flip))


def across(value, flip):
    return lax.ppermute(value, "dp", [(k, k ^ flip) for k in range(N_DP)])


def add(*parts):
    return sum(p.astype(F32) for p in parts).astype(BF16)


def add_rows(value, more, start):
    rows = more.shape[0]
    return lax.dynamic_update_slice(value, add(value[start : start + rows], more), (start, 0))


def centre(wide):
    centred = wide - jnp.mean(wide, axis=-1, keepdims=True)
    factor = lax.rsqrt(jnp.mean(centred * centred, axis=-1, keepdims=True) + EPS)
    return centred * factor, factor


def norm_kernel(x_ref, gain_ref, bias_ref, out_ref):
    hat, _ = centre(x_ref[...].astype(F32))
    out_ref[...] = (hat * gain_ref[...] + bias_ref[...]).astype(BF16)


def norm_rows(x, gain, bias):
    return pl.pallas_call(
        norm_kernel,
        out_shape=jax.ShapeDtypeStruct(x.shape, BF16),
        compiler_params=pltpu.CompilerParams(vmem_limit_bytes=VMEM_LIMIT),
        cost_estimate=TINY,
        name="norm_rows",
    )(x, gain, bias)


def patch_kernel(x_ref, gain_ref, own_ref, got1_ref, got3_ref, out_ref):
    hat, factor = centre(x_ref[...].astype(F32))
    grad = own_ref[0:BLK].astype(F32) + got1_ref[...].astype(F32) + got3_ref[...].astype(F32)
    scaled = grad * gain_ref[...]
    out_ref[...] = (
        factor
        * (
            scaled
            - jnp.mean(scaled, axis=-1, keepdims=True)
            - hat * jnp.mean(scaled * hat, axis=-1, keepdims=True)
        )
    ).astype(BF16)


def patch_rows(x, gain, *pieces):
    return pl.pallas_call(
        patch_kernel,
        out_shape=jax.ShapeDtypeStruct(x.shape, BF16),
        compiler_params=pltpu.CompilerParams(vmem_limit_bytes=VMEM_LIMIT),
        cost_estimate=TINY,
        name="patch_rows",
    )(x, gain, *pieces)


def shard_labels(counts_ref, shard, shape, dim):
    first = (shard // 2) * 2
    merged = counts_ref[first] > BLK
    image = jnp.where(merged, first, shard)
    count = counts_ref[image]
    offset = lax.broadcasted_iota(jnp.int32, shape, dim) + BLK * (shard - image)
    return jnp.where(offset < count, image, -1 - shard)


def whole(w_ref):
    return jnp.concatenate([w_ref[part] for part in range(3)], axis=1)


def nt(left, right):
    return lax.dot_general(left, right, (((1,), (1,)), ((), ())), preferred_element_type=F32)


def tn(left, right):
    return lax.dot_general(left, right, (((0,), (0,)), ((), ())), preferred_element_type=F32)


def back(grad, hat, factor, gain):
    scaled = grad * gain
    return factor * (
        scaled
        - jnp.mean(scaled, axis=-1, keepdims=True)
        - hat * jnp.mean(scaled * hat, axis=-1, keepdims=True)
    )


def quad_kernel(n_slots, n_outs, first, meta, counts, *refs):
    refs = list(refs)
    slots = [refs.pop(0) for _ in range(n_slots)]
    w_ref, up_ref, qg_ref, kg_ref = [refs.pop(0) for _ in range(4)]
    if not first:
        norms_in, terms_in, _ = [refs.pop(0) for _ in range(3)]
    att_ref = refs.pop(0)
    dnormed = [refs.pop(0) for _ in range(n_outs)]
    dproj_ref, norms_ref, terms_ref, proj, dbuf, abuf, sems = refs
    core = meta[0]
    places = [0, 1 + core, 2 - core, 3]

    def rows_of(place):
        return pl.ds(pl.multiple_of(place * BLK, BLK), BLK)

    def taken(refs, side):
        start = 0
        found = []
        for ref in refs:
            if start // (2 * BLK) == side:
                found.append((ref, start % (2 * BLK)))
            start += ref.shape[0]
        return found

    def rows_in(side):
        return jnp.concatenate([ref[...] for ref, _ in taken(slots, side)], axis=0)

    for side in range(2):
        result = jnp.dot(rows_in(side), whole(w_ref), preferred_element_type=F32)
        for k in range(2):
            proj[rows_of(places[2 * side + k]), :] = result[k * BLK : (k + 1) * BLK]

    scale = 1.0 / math.sqrt(HDIM)
    q_terms = [None, None]
    k_terms = [None, None]
    copies = []
    for pair in range(2):
        shards = [meta[1 + 2 * pair + k] for k in range(2)]
        columns = jnp.concatenate([shard_labels(counts, s, (BLK, 1), 0) for s in shards], axis=0)
        across = jnp.concatenate([shard_labels(counts, s, (1, BLK), 1) for s in shards], axis=1)
        same = columns == across
        rows = slice(pair * 2 * BLK, (pair + 1) * 2 * BLK)
        for head in range(2):
            cols = slice(head * HDIM, (head + 1) * HDIM)
            q_gain = qg_ref[:, cols]
            k_gain = kg_ref[:, cols]
            q_hat, q_factor = centre(proj[rows, head * HDIM : (head + 1) * HDIM])
            k_hat, k_factor = centre(proj[rows, (2 + head) * HDIM : (3 + head) * HDIM])
            value = proj[rows, (4 + head) * HDIM : (5 + head) * HDIM].astype(BF16)
            q_s = (q_hat * q_gain).astype(BF16)
            k_s = (k_hat * k_gain).astype(BF16)
            grad = jnp.concatenate([up_ref[rows_of(s), cols] for s in shards], axis=0)
            weights = jnp.where(same, jnp.exp(nt(q_s, k_s) * scale), 0.0)
            probs = weights * (1.0 / jnp.sum(weights, axis=-1, keepdims=True))
            probs_b = probs.astype(BF16)
            abuf[rows, cols] = jnp.dot(probs_b, value, preferred_element_type=F32).astype(BF16)
            dprob = nt(grad, value)
            inner = jnp.sum(probs * dprob, axis=-1, keepdims=True)
            dscore = (probs * (dprob - inner) * scale).astype(BF16)
            dvalue = tn(probs_b, grad)
            dquery = jnp.dot(dscore, k_s, preferred_element_type=F32)
            dkey = tn(dscore, q_s)
            q_term = jnp.sum(dquery * q_hat, axis=0, keepdims=True)
            k_term = jnp.sum(dkey * k_hat, axis=0, keepdims=True)
            q_terms[head] = q_term if pair == 0 else q_terms[head] + q_term
            k_terms[head] = k_term if pair == 0 else k_terms[head] + k_term
            dbuf[rows, head * HDIM : (head + 1) * HDIM] = back(dquery, q_hat, q_factor, q_gain).astype(BF16)
            dbuf[rows, (2 + head) * HDIM : (3 + head) * HDIM] = back(dkey, k_hat, k_factor, k_gain).astype(BF16)
            dbuf[rows, (4 + head) * HDIM : (5 + head) * HDIM] = dvalue.astype(BF16)
        for k in range(2):
            place = 2 * pair + k
            copy = pltpu.make_async_copy(
                abuf.at[pl.ds(place * BLK, BLK)], att_ref.at[rows_of(shards[k])], sems.at[place]
            )
            copy.start()
            copies.append(copy)
    terms = jnp.concatenate(q_terms + k_terms, axis=1)
    terms_ref[...] = terms if first else terms_in[...] + terms

    for side in range(2):
        part = jnp.concatenate([dbuf[rows_of(places[2 * side + k]), :] for k in range(2)], axis=0)
        dproj_ref[side * 2 * BLK : (side + 1) * 2 * BLK] = part
        result = nt(part, whole(w_ref))
        sums = jnp.concatenate(
            [
                jnp.sum(result * rows_in(side).astype(F32), axis=0, keepdims=True),
                jnp.sum(result, axis=0, keepdims=True),
            ],
            axis=1,
        )
        if side == 0:
            norms_ref[...] = sums if first else norms_in[...] + sums
        else:
            norms_ref[...] += sums
        for ref, start in taken(dnormed, side):
            ref[...] = result[start : start + ref.shape[0]].astype(BF16)
    for copy in copies:
        copy.wait()


def quad(meta, counts, slots, outs, weight, upstream, q_gain, k_gain, before):
    length, heads = upstream.shape
    width = weight.shape[1]
    cols = 3 * heads
    first = before is None
    vmem = pl.BlockSpec(memory_space=pltpu.VMEM)
    smem = pl.BlockSpec(memory_space=pltpu.SMEM)
    anywhere = pl.BlockSpec(memory_space=pl.ANY)
    operands = [meta, counts, *slots, weight, upstream, q_gain, k_gain]
    in_specs = [smem, smem] + [vmem] * (len(operands) - 2)
    aliases = {}
    if not first:
        operands += before
        in_specs += [vmem, vmem, anywhere]
        aliases = {len(operands) - 1: 0}
    found = pl.pallas_call(
        functools.partial(quad_kernel, len(slots), len(outs), first),
        in_specs=in_specs,
        out_specs=[anywhere] + [vmem] * (len(outs) + 3),
        out_shape=[jax.ShapeDtypeStruct((length, heads), BF16)]
        + [jax.ShapeDtypeStruct((rows, width), BF16) for rows in outs]
        + [
            jax.ShapeDtypeStruct((4 * BLK, cols), BF16),
            jax.ShapeDtypeStruct((1, 2 * width), F32),
            jax.ShapeDtypeStruct((1, 2 * heads), F32),
        ],
        scratch_shapes=[
            pltpu.VMEM((4 * BLK, cols), F32),
            pltpu.VMEM((4 * BLK, cols), BF16),
            pltpu.VMEM((4 * BLK, heads), BF16),
            pltpu.SemaphoreType.DMA((4,)),
        ],
        input_output_aliases=aliases,
        compiler_params=pltpu.CompilerParams(vmem_limit_bytes=VMEM_LIMIT),
        cost_estimate=TINY,
        name="quad",
    )(*operands)
    attention, *dnormed, dproj, norms, terms = found
    return [norms, terms, attention], dnormed, dproj


def weight_kernel(n_rows, place, *refs):
    rows = refs[:n_rows]
    dprojs = refs[n_rows : n_rows + 4]
    out_ref = refs[-1]
    left = jnp.concatenate([ref[...] for ref in rows], axis=0)
    right = jnp.concatenate([ref[...] for ref in dprojs], axis=0)
    out_ref[...] = tn(left, right).astype(BF16)


def weight_grads(dp, rows, dprojs, odd):
    width = rows[0].shape[1]
    cols = dprojs[0].shape[1]
    tile = width // N_DP
    steps = N_DP // 2
    return pl.pallas_call(
        functools.partial(weight_kernel, len(rows)),
        grid_spec=pltpu.PrefetchScalarGridSpec(
            num_scalar_prefetch=1,
            grid=(steps,),
            in_specs=[
                pl.BlockSpec((r.shape[0], tile), lambda i, place: (0, place[0] ^ (2 * i + odd))) for r in rows
            ]
            + [pl.BlockSpec(d.shape, lambda i, place: (0, 0)) for d in dprojs],
            out_specs=pl.BlockSpec((tile, cols), lambda i, place: (i, 0)),
        ),
        out_shape=jax.ShapeDtypeStruct((steps * tile, cols), BF16),
        compiler_params=pltpu.CompilerParams(vmem_limit_bytes=VMEM_LIMIT),
        cost_estimate=TINY,
        name="weight_grads",
    )(dp, *rows, *dprojs)


def share_kernel(factor, own_ref, got1_ref, got3_ref, out_ref):
    cols = out_ref.shape[2]
    total = own_ref[0 : got1_ref.shape[0]].astype(F32) + got1_ref[...].astype(F32)
    total = (total + got3_ref[...].astype(F32)) * factor
    for part in range(3):
        out_ref[part] = total[:, part * cols : (part + 1) * cols]


def weight_out(own, got1, got3, factor):
    rows, cols = got1.shape
    return pl.pallas_call(
        functools.partial(share_kernel, factor),
        out_shape=jax.ShapeDtypeStruct((3, rows, cols // 3), F32),
        compiler_params=pltpu.CompilerParams(vmem_limit_bytes=VMEM_LIMIT),
        cost_estimate=TINY,
        name="weight_out",
    )(own, got1, got3).transpose(1, 0, 2)


def quad_meta(core, tensor, i, j):
    found = [core]
    for place in range(4):
        straight = (i + place // 2) * 4 + j + place % 2
        turned = (j + place // 2) * 4 + i + place % 2
        found.append(tensor ^ jnp.where(core == 0, straight, turned))
    return jnp.stack(found).astype(jnp.int32)


def total_over(value, axis, flips):
    size = lax.axis_size(axis)
    for flip in flips:
        value = value + lax.ppermute(value, axis, [(k, k ^ flip) for k in range(size)])
    return value


def together(*values):
    return lax.optimization_barrier(values)


def together(*values):
    return lax.optimization_barrier(values)


def body(patches, counts, norm_gain, norm_bias, qkv_weight, query_gain, key_gain, upstream):
    width = patches.shape[2]
    local = qkv_weight.shape[2]
    length = upstream.shape[1]
    factor = 1.0 / math.sqrt(lax.axis_size("dp") * length)
    dp = lax.axis_index("dp")
    core = dp % 2
    tensor = lax.axis_index("tensor")
    gain = norm_gain.reshape(1, width)
    bias = norm_bias.reshape(1, width)
    weight = qkv_weight.transpose(1, 0, 2)
    own_rows = patches[0]
    half = BLK // 2

    own = norm_rows(own_rows, gain, bias)
    near, next3 = swap(own, 1, 1), swap(own, 1, 3)
    metas = [quad_meta(core, tensor, i, j) for i, j in ((0, 0), (2, 0), (0, 2), (2, 2))]
    near, next3, *metas = together(near, next3, *metas)
    top, bottom = swap(next3[:half], 1, 1), swap(near[half:], 1, 3)
    a0 = jnp.concatenate([own, near], axis=0)
    a1, a3 = swap(a0, 2, 1), swap(a0, 2, 3)
    b0 = jnp.concatenate([top, bottom, next3], axis=0)
    b1, b3 = swap(b0, 2, 1), swap(b0, 2, 3)
    a2_top, a2_bottom = swap(a3[:BLK], 2, 1), swap(a1[BLK:], 2, 3)

    def run(meta, slots, outs, before):
        return quad(
            meta,
            counts[0],
            slots,
            outs,
            weight,
            upstream[0],
            query_gain.reshape(1, local),
            key_gain.reshape(1, local),
            before,
        )

    near_outs, far_outs = [2 * BLK, 2 * BLK], [BLK, BLK, 2 * BLK]
    state, (da0, da1), dproj0 = run(metas[0], [a0, a1], near_outs, None)
    state[0], b1, b3 = together(state[0], b1, b3)
    b2_top, b2_bottom = swap(b3[:BLK], 2, 1), swap(b1[BLK:], 2, 3)
    state, (db0, db1), dproj2 = run(metas[2], [b0, b1], near_outs, state)
    state[0], a2_top, a2_bottom, a3 = together(state[0], a2_top, a2_bottom, a3)
    state, (da2_top, da2_bottom, da3), dproj1 = run(metas[1], [a2_top, a2_bottom, a3], far_outs, state)
    fa_top, fa_bottom = swap(da2_top, 2, 3), swap(da2_bottom, 2, 1)
    state[0], b2_top, b2_bottom = together(state[0], b2_top, b2_bottom)
    state, (db2_top, db2_bottom, db3), dproj3 = run(metas[3], [b2_top, b2_bottom, b3], far_outs, state)
    norms, terms, attention = state

    norms, fa_top, fa_bottom = together(norms, fa_top, fa_bottom)
    da1, da3 = add_rows(da1, fa_top, 0), add_rows(da3, fa_bottom, BLK)
    norms, da1, da3, db2_top, db2_bottom, dproj3 = together(norms, da1, da3, db2_top, db2_bottom, dproj3)
    fb_top, fb_bottom = swap(db2_top, 2, 3), swap(db2_bottom, 2, 1)
    ga1, ga3 = swap(da1, 2, 1), swap(da3, 2, 3)
    rows = [a0, a1, b0, b1, a2_top, a2_bottom, a3, b2_top, b2_bottom, b3]
    place = dp.astype(jnp.int32).reshape(1)
    dprojs = [dproj0, dproj2, dproj1, dproj3]
    other = weight_grads(place, rows, dprojs, 1)
    mine = weight_grads(place, rows, dprojs, 0)
    small = total_over(jnp.concatenate([norms, terms], axis=1), "dp", (1, 2))
    other, mine, small, fb_top, fb_bottom, ga1, ga3 = together(
        other, mine, small, fb_top, fb_bottom, ga1, ga3
    )

    db1, db3 = add_rows(db1, fb_top, 0), add_rows(db3, fb_bottom, BLK)
    db1, db3, other, mine, small = together(db1, db3, other, mine, small)
    gb1, gb3 = swap(db1, 2, 1), swap(db3, 2, 3)
    from_core = across(other, 1)
    small = total_over(small, "dp", (4,))
    small, terms = small[:, : 2 * width], small[:, 2 * width :]
    small = total_over(small, "tensor", (1,))
    r_near = add(da0, ga1, ga3)
    both = add(mine, from_core)
    share = both.shape[0] // 4
    cut = share // 2
    y_top, y_bottom = across(both[2 * share : 2 * share + cut], 6), across(both[2 * share + cut : 3 * share], 2)
    y_top, y_bottom, small, gb1, gb3, r_near = together(y_top, y_bottom, small, gb1, gb3, r_near)

    r_far = add(db0, gb1, gb3)
    y1 = add_rows(both[share : 2 * share], y_top, 0)
    y3 = add_rows(both[3 * share :], y_bottom, cut)
    r_far, y1, y3, small = together(r_far, y1, y3, small)
    u_top, u_bottom = swap(r_far[:half], 1, 3), swap(r_far[half:BLK], 1, 1)
    z1, z3 = across(y1, 2), across(y3, 6)
    small = total_over(small, "tensor", (2,))
    small, u_top, u_bottom = together(small, u_top, u_bottom)
    v1, v3 = add_rows(r_near[BLK:], u_top, 0), add_rows(r_far[BLK:], u_bottom, half)
    small, v1, v3 = together(small, v1, v3)
    v1, v3 = swap(v1, 1, 1), swap(v3, 1, 3)
    small = total_over(small, "tensor", (4,))
    small, v1, v3, z1, z3 = together(small, v1, v3, z1, z3)
    small = total_over(small, "tensor", (8,)) * factor
    weight_grad = weight_out(both, z1, z3, factor)
    patch_grad = patch_rows(own_rows, gain, r_near, v1, v3)
    shift = small[:, width : 2 * width]
    gain_grad = (small[:, :width] - bias * shift) / gain
    return (
        attention.reshape(1, length, local),
        patch_grad[None],
        weight_grad,
        gain_grad[0],
        shift[0],
        terms[0, :local] * factor,
        terms[0, local:] * factor,
    )


def solution(mesh):
    in_specs = (
        P("dp", "tensor", None),
        P("dp", None),
        P(),
        P(),
        P(None, None, "tensor"),
        P("tensor"),
        P("tensor"),
        P("dp", None, "tensor"),
    )
    out_specs = (
        P("dp", None, "tensor"),
        P("dp", "tensor", None),
        P("dp", None, "tensor"),
        P(),
        P(),
        P("tensor"),
        P("tensor"),
    )
    return jax.shard_map(body, mesh=mesh, in_specs=in_specs, out_specs=out_specs, check_vma=False)
```

```python
import functools
import math

import jax
import jax.numpy as jnp
from jax import lax
from jax.experimental import pallas as pl
from jax.experimental.pallas import tpu as pltpu
from jax.sharding import PartitionSpec as P

HDIM = 128
BLK = 128
EPS = 1e-06
AXES = ("dp", "tensor")
N_DP = 8
N_T = 16
VMEM_LIMIT = 22 * 1024 * 1024
TINY = pl.CostEstimate(flops=1000, bytes_accessed=1000, transcendentals=0)
F32 = jnp.float32
BF16 = jnp.bfloat16


def ring_pairs(ring, flip):
    pairs = []
    for dp in range(N_DP):
        for t in range(N_T):
            along_x = (dp % 2 == 0) == (ring == 1)
            pairs.append((dp * N_T + t, dp * N_T + (t ^ (flip if along_x else 4 * flip))))
    return pairs


def swap(value, ring, flip):
    return lax.ppermute(value, AXES, ring_pairs(ring, flip))


def across(value, flip):
    return lax.ppermute(value, "dp", [(k, k ^ flip) for k in range(N_DP)])


def add(*parts):
    return sum(p.astype(F32) for p in parts).astype(BF16)


def add_rows(value, more, start):
    rows = more.shape[0]
    return lax.dynamic_update_slice(value, add(value[start : start + rows], more), (start, 0))


def centre(wide):
    centred = wide - jnp.mean(wide, axis=-1, keepdims=True)
    factor = lax.rsqrt(jnp.mean(centred * centred, axis=-1, keepdims=True) + EPS)
    return centred * factor, factor


def norm_kernel(x_ref, gain_ref, bias_ref, out_ref):
    hat, _ = centre(x_ref[...].astype(F32))
    out_ref[...] = (hat * gain_ref[...] + bias_ref[...]).astype(BF16)


def norm_rows(x, gain, bias):
    return pl.pallas_call(
        norm_kernel,
        out_shape=jax.ShapeDtypeStruct(x.shape, BF16),
        compiler_params=pltpu.CompilerParams(vmem_limit_bytes=VMEM_LIMIT),
        cost_estimate=TINY,
        name="norm_rows",
    )(x, gain, bias)


def patch_kernel(x_ref, gain_ref, own_ref, got1_ref, got2_ref, got3_ref, out_ref):
    hat, factor = centre(x_ref[...].astype(F32))
    near = own_ref[0:BLK].astype(F32) + got1_ref[...].astype(F32)
    scaled = (near + got2_ref[...].astype(F32) + got3_ref[...].astype(F32)) * gain_ref[...]
    out_ref[...] = (
        factor
        * (
            scaled
            - jnp.mean(scaled, axis=-1, keepdims=True)
            - hat * jnp.mean(scaled * hat, axis=-1, keepdims=True)
        )
    ).astype(BF16)


def patch_rows(x, gain, *pieces):
    return pl.pallas_call(
        patch_kernel,
        out_shape=jax.ShapeDtypeStruct(x.shape, BF16),
        compiler_params=pltpu.CompilerParams(vmem_limit_bytes=VMEM_LIMIT),
        cost_estimate=TINY,
        name="patch_rows",
    )(x, gain, *pieces)


def shard_labels(counts_ref, shard, shape, dim):
    first = (shard // 2) * 2
    merged = counts_ref[first] > BLK
    image = jnp.where(merged, first, shard)
    count = counts_ref[image]
    offset = lax.broadcasted_iota(jnp.int32, shape, dim) + BLK * (shard - image)
    return jnp.where(offset < count, image, -1 - shard)


def whole(w_ref):
    return jnp.concatenate([w_ref[part] for part in range(3)], axis=1)


def nt(left, right):
    return lax.dot_general(left, right, (((1,), (1,)), ((), ())), preferred_element_type=F32)


def tn(left, right):
    return lax.dot_general(left, right, (((0,), (0,)), ((), ())), preferred_element_type=F32)


def back(grad, hat, factor, gain):
    scaled = grad * gain
    return factor * (
        scaled
        - jnp.mean(scaled, axis=-1, keepdims=True)
        - hat * jnp.mean(scaled * hat, axis=-1, keepdims=True)
    )


def quad_kernel(n_slots, n_outs, first, meta, counts, *refs):
    refs = list(refs)
    slots = [refs.pop(0) for _ in range(n_slots)]
    w_ref, up_ref, qg_ref, kg_ref = [refs.pop(0) for _ in range(4)]
    if not first:
        norms_in, terms_in, _ = [refs.pop(0) for _ in range(3)]
    att_ref = refs.pop(0)
    dnormed = [refs.pop(0) for _ in range(n_outs)]
    dproj_ref, norms_ref, terms_ref, proj, dbuf, abuf, sems = refs
    core = meta[0]
    places = [0, 1 + core, 2 - core, 3]

    def rows_of(place):
        return pl.ds(pl.multiple_of(place * BLK, BLK), BLK)

    def taken(refs, side):
        start = 0
        found = []
        for ref in refs:
            if start // (2 * BLK) == side:
                found.append((ref, start % (2 * BLK)))
            start += ref.shape[0]
        return found

    def rows_in(side):
        return jnp.concatenate([ref[...] for ref, _ in taken(slots, side)], axis=0)

    for side in range(2):
        result = jnp.dot(rows_in(side), whole(w_ref), preferred_element_type=F32)
        for k in range(2):
            proj[rows_of(places[2 * side + k]), :] = result[k * BLK : (k + 1) * BLK]

    scale = 1.0 / math.sqrt(HDIM)
    q_terms = [None, None]
    k_terms = [None, None]
    copies = []
    for pair in range(2):
        shards = [meta[1 + 2 * pair + k] for k in range(2)]
        columns = jnp.concatenate([shard_labels(counts, s, (BLK, 1), 0) for s in shards], axis=0)
        across = jnp.concatenate([shard_labels(counts, s, (1, BLK), 1) for s in shards], axis=1)
        same = columns == across
        rows = slice(pair * 2 * BLK, (pair + 1) * 2 * BLK)
        for head in range(2):
            cols = slice(head * HDIM, (head + 1) * HDIM)
            q_gain = qg_ref[:, cols]
            k_gain = kg_ref[:, cols]
            q_hat, q_factor = centre(proj[rows, head * HDIM : (head + 1) * HDIM])
            k_hat, k_factor = centre(proj[rows, (2 + head) * HDIM : (3 + head) * HDIM])
            value = proj[rows, (4 + head) * HDIM : (5 + head) * HDIM].astype(BF16)
            q_s = (q_hat * q_gain).astype(BF16)
            k_s = (k_hat * k_gain).astype(BF16)
            grad = jnp.concatenate([up_ref[rows_of(s), cols] for s in shards], axis=0)
            weights = jnp.where(same, jnp.exp(nt(q_s, k_s) * scale), 0.0)
            probs = weights * (1.0 / jnp.sum(weights, axis=-1, keepdims=True))
            probs_b = probs.astype(BF16)
            abuf[rows, cols] = jnp.dot(probs_b, value, preferred_element_type=F32).astype(BF16)
            dprob = nt(grad, value)
            inner = jnp.sum(probs * dprob, axis=-1, keepdims=True)
            dscore = (probs * (dprob - inner) * scale).astype(BF16)
            dvalue = tn(probs_b, grad)
            dquery = jnp.dot(dscore, k_s, preferred_element_type=F32)
            dkey = tn(dscore, q_s)
            q_term = jnp.sum(dquery * q_hat, axis=0, keepdims=True)
            k_term = jnp.sum(dkey * k_hat, axis=0, keepdims=True)
            q_terms[head] = q_term if pair == 0 else q_terms[head] + q_term
            k_terms[head] = k_term if pair == 0 else k_terms[head] + k_term
            dbuf[rows, head * HDIM : (head + 1) * HDIM] = back(dquery, q_hat, q_factor, q_gain).astype(BF16)
            dbuf[rows, (2 + head) * HDIM : (3 + head) * HDIM] = back(dkey, k_hat, k_factor, k_gain).astype(BF16)
            dbuf[rows, (4 + head) * HDIM : (5 + head) * HDIM] = dvalue.astype(BF16)
        for k in range(2):
            place = 2 * pair + k
            copy = pltpu.make_async_copy(
                abuf.at[pl.ds(place * BLK, BLK)], att_ref.at[rows_of(shards[k])], sems.at[place]
            )
            copy.start()
            copies.append(copy)
    terms = jnp.concatenate(q_terms + k_terms, axis=1)
    terms_ref[...] = terms if first else terms_in[...] + terms

    for side in range(2):
        part = jnp.concatenate([dbuf[rows_of(places[2 * side + k]), :] for k in range(2)], axis=0)
        dproj_ref[side * 2 * BLK : (side + 1) * 2 * BLK] = part
        result = nt(part, whole(w_ref))
        sums = jnp.concatenate(
            [
                jnp.sum(result * rows_in(side).astype(F32), axis=0, keepdims=True),
                jnp.sum(result, axis=0, keepdims=True),
            ],
            axis=1,
        )
        if side == 0:
            norms_ref[...] = sums if first else norms_in[...] + sums
        else:
            norms_ref[...] += sums
        for ref, start in taken(dnormed, side):
            ref[...] = result[start : start + ref.shape[0]].astype(BF16)
    for copy in copies:
        copy.wait()


def quad(meta, counts, slots, outs, weight, upstream, q_gain, k_gain, before):
    length, heads = upstream.shape
    width = weight.shape[1]
    cols = 3 * heads
    first = before is None
    vmem = pl.BlockSpec(memory_space=pltpu.VMEM)
    smem = pl.BlockSpec(memory_space=pltpu.SMEM)
    anywhere = pl.BlockSpec(memory_space=pl.ANY)
    operands = [meta, counts, *slots, weight, upstream, q_gain, k_gain]
    in_specs = [smem, smem] + [vmem] * (len(operands) - 2)
    aliases = {}
    if not first:
        operands += before
        in_specs += [vmem, vmem, anywhere]
        aliases = {len(operands) - 1: 0}
    found = pl.pallas_call(
        functools.partial(quad_kernel, len(slots), len(outs), first),
        in_specs=in_specs,
        out_specs=[anywhere] + [vmem] * (len(outs) + 3),
        out_shape=[jax.ShapeDtypeStruct((length, heads), BF16)]
        + [jax.ShapeDtypeStruct((rows, width), BF16) for rows in outs]
        + [
            jax.ShapeDtypeStruct((4 * BLK, cols), BF16),
            jax.ShapeDtypeStruct((1, 2 * width), F32),
            jax.ShapeDtypeStruct((1, 2 * heads), F32),
        ],
        scratch_shapes=[
            pltpu.VMEM((4 * BLK, cols), F32),
            pltpu.VMEM((4 * BLK, cols), BF16),
            pltpu.VMEM((4 * BLK, heads), BF16),
            pltpu.SemaphoreType.DMA((4,)),
        ],
        input_output_aliases=aliases,
        compiler_params=pltpu.CompilerParams(vmem_limit_bytes=VMEM_LIMIT),
        cost_estimate=TINY,
        name="quad",
    )(*operands)
    attention, *dnormed, dproj, norms, terms = found
    return [norms, terms, attention], dnormed, dproj


def weight_kernel(n_rows, place, *refs):
    rows = refs[:n_rows]
    dprojs = refs[n_rows : n_rows + 4]
    out_ref = refs[-1]
    left = jnp.concatenate([ref[...] for ref in rows], axis=0)
    right = jnp.concatenate([ref[...] for ref in dprojs], axis=0)
    out_ref[...] = tn(left, right).astype(BF16)


def weight_grads(dp, rows, dprojs, odd):
    width = rows[0].shape[1]
    cols = dprojs[0].shape[1]
    tile = width // N_DP
    steps = N_DP // 2
    return pl.pallas_call(
        functools.partial(weight_kernel, len(rows)),
        grid_spec=pltpu.PrefetchScalarGridSpec(
            num_scalar_prefetch=1,
            grid=(steps,),
            in_specs=[
                pl.BlockSpec((r.shape[0], tile), lambda i, place: (0, place[0] ^ (2 * i + odd))) for r in rows
            ]
            + [pl.BlockSpec(d.shape, lambda i, place: (0, 0)) for d in dprojs],
            out_specs=pl.BlockSpec((tile, cols), lambda i, place: (i, 0)),
        ),
        out_shape=jax.ShapeDtypeStruct((steps * tile, cols), BF16),
        compiler_params=pltpu.CompilerParams(vmem_limit_bytes=VMEM_LIMIT),
        cost_estimate=TINY,
        name="weight_grads",
    )(dp, *rows, *dprojs)


def share_kernel(factor, own_ref, got1_ref, got3_ref, out_ref):
    cols = out_ref.shape[2]
    total = own_ref[0 : got1_ref.shape[0]].astype(F32) + got1_ref[...].astype(F32)
    total = (total + got3_ref[...].astype(F32)) * factor
    for part in range(3):
        out_ref[part] = total[:, part * cols : (part + 1) * cols]


def weight_out(own, got1, got3, factor):
    rows, cols = got1.shape
    return pl.pallas_call(
        functools.partial(share_kernel, factor),
        out_shape=jax.ShapeDtypeStruct((3, rows, cols // 3), F32),
        compiler_params=pltpu.CompilerParams(vmem_limit_bytes=VMEM_LIMIT),
        cost_estimate=TINY,
        name="weight_out",
    )(own, got1, got3).transpose(1, 0, 2)


def quad_meta(core, tensor, i, j):
    found = [core]
    for place in range(4):
        straight = (i + place // 2) * 4 + j + place % 2
        turned = (j + place // 2) * 4 + i + place % 2
        found.append(tensor ^ jnp.where(core == 0, straight, turned))
    return jnp.stack(found).astype(jnp.int32)


def total_over(value, axis, flips):
    size = lax.axis_size(axis)
    for flip in flips:
        value = value + lax.ppermute(value, axis, [(k, k ^ flip) for k in range(size)])
    return value


def gather_sum(value, flips):
    return value + sum(lax.ppermute(value, "tensor", [(k, k ^ flip) for k in range(N_T)]) for flip in flips)


def together(*values):
    return lax.optimization_barrier(values)


def gather_sum(value, flips):
    return value + sum(lax.ppermute(value, "tensor", [(k, k ^ flip) for k in range(N_T)]) for flip in flips)


def together(*values):
    return lax.optimization_barrier(values)


def body(patches, counts, norm_gain, norm_bias, qkv_weight, query_gain, key_gain, upstream):
    width = patches.shape[2]
    local = qkv_weight.shape[2]
    length = upstream.shape[1]
    factor = 1.0 / math.sqrt(lax.axis_size("dp") * length)
    dp = lax.axis_index("dp")
    core = dp % 2
    tensor = lax.axis_index("tensor")
    gain = norm_gain.reshape(1, width)
    bias = norm_bias.reshape(1, width)
    weight = qkv_weight.transpose(1, 0, 2)
    own_rows = patches[0]
    half = BLK // 2

    own = norm_rows(own_rows, gain, bias)
    near, next3 = swap(own, 1, 1), swap(own, 1, 3)
    metas = [quad_meta(core, tensor, i, j) for i, j in ((0, 0), (2, 0), (0, 2), (2, 2))]
    near, next3, *metas = together(near, next3, *metas)
    top, bottom = swap(next3[:half], 1, 1), swap(near[half:], 1, 3)
    a0 = jnp.concatenate([own, near], axis=0)
    a1, a3 = swap(a0, 2, 1), swap(a0, 2, 3)
    b0 = jnp.concatenate([top, bottom, next3], axis=0)
    b1, b3 = swap(b0, 2, 1), swap(b0, 2, 3)
    a2_top, a2_bottom = swap(a3[:BLK], 2, 1), swap(a1[BLK:], 2, 3)

    def run(meta, slots, outs, before):
        return quad(
            meta,
            counts[0],
            slots,
            outs,
            weight,
            upstream[0],
            query_gain.reshape(1, local),
            key_gain.reshape(1, local),
            before,
        )

    near_outs, far_outs = [2 * BLK, 2 * BLK], [BLK, BLK, 2 * BLK]
    state, (da0, da1), dproj0 = run(metas[0], [a0, a1], near_outs, None)
    state[0], b1, b3 = together(state[0], b1, b3)
    b2_top, b2_bottom = swap(b3[:BLK], 2, 1), swap(b1[BLK:], 2, 3)
    state, (db0, db1), dproj2 = run(metas[2], [b0, b1], near_outs, state)
    state[0], a2_top, a2_bottom, a3 = together(state[0], a2_top, a2_bottom, a3)
    state, (da2_top, da2_bottom, da3), dproj1 = run(metas[1], [a2_top, a2_bottom, a3], far_outs, state)
    fa_top, fa_bottom = swap(da2_top, 2, 3), swap(da2_bottom, 2, 1)
    state[0], b2_top, b2_bottom = together(state[0], b2_top, b2_bottom)
    state, (db2_top, db2_bottom, db3), dproj3 = run(metas[3], [b2_top, b2_bottom, b3], far_outs, state)
    norms, terms, attention = state

    norms, fa_top, fa_bottom = together(norms, fa_top, fa_bottom)
    da1, da3 = add_rows(da1, fa_top, 0), add_rows(da3, fa_bottom, BLK)
    norms, da1, da3, db2_top, db2_bottom, dproj3 = together(norms, da1, da3, db2_top, db2_bottom, dproj3)
    fb_top, fb_bottom = swap(db2_top, 2, 3), swap(db2_bottom, 2, 1)
    ga1, ga3 = swap(da1, 2, 1), swap(da3, 2, 3)
    rows = [a0, a1, b0, b1, a2_top, a2_bottom, a3, b2_top, b2_bottom, b3]
    place = dp.astype(jnp.int32).reshape(1)
    dprojs = [dproj0, dproj2, dproj1, dproj3]
    other = weight_grads(place, rows, dprojs, 1)
    mine = weight_grads(place, rows, dprojs, 0)
    small = total_over(jnp.concatenate([norms, terms], axis=1), "dp", (1, 2))
    other, mine, small, fb_top, fb_bottom, ga1, ga3 = together(
        other, mine, small, fb_top, fb_bottom, ga1, ga3
    )

    db1, db3 = add_rows(db1, fb_top, 0), add_rows(db3, fb_bottom, BLK)
    db1, db3, other, mine, small = together(db1, db3, other, mine, small)
    gb1, gb3 = swap(db1, 2, 1), swap(db3, 2, 3)
    from_core = across(other, 1)
    small = total_over(small, "dp", (4,))
    small, terms = small[:, : 2 * width], small[:, 2 * width :]
    small = gather_sum(small, (1, 2, 3))
    r_near = add(da0, ga1, ga3)
    both = add(mine, from_core)
    share = both.shape[0] // 4
    cut = share // 2
    y_top, y_bottom = across(both[2 * share : 2 * share + cut], 6), across(both[2 * share + cut : 3 * share], 2)
    y_top, y_bottom, small, gb1, gb3, r_near = together(y_top, y_bottom, small, gb1, gb3, r_near)

    r_far = add(db0, gb1, gb3)
    y1 = add_rows(both[share : 2 * share], y_top, 0)
    y3 = add_rows(both[3 * share :], y_bottom, cut)
    r_far, y1, y3, small = together(r_far, y1, y3, small)
    v2, v1, v3 = swap(r_far[:BLK], 1, 2), swap(r_near[BLK:], 1, 1), swap(r_far[BLK:], 1, 3)
    z1, z3 = across(y1, 2), across(y3, 6)
    small, v1, v2, v3, z1, z3 = together(small, v1, v2, v3, z1, z3)
    small = gather_sum(small, (4, 8, 12)) * factor
    patch_grad = patch_rows(own_rows, gain, r_near, v1, v2, v3)
    weight_grad = weight_out(both, z1, z3, factor)
    shift = small[:, width : 2 * width]
    gain_grad = (small[:, :width] - bias * shift) / gain
    return (
        attention.reshape(1, length, local),
        patch_grad[None],
        weight_grad,
        gain_grad[0],
        shift[0],
        terms[0, :local] * factor,
        terms[0, local:] * factor,
    )


def solution(mesh):
    in_specs = (
        P("dp", "tensor", None),
        P("dp", None),
        P(),
        P(),
        P(None, None, "tensor"),
        P("tensor"),
        P("tensor"),
        P("dp", None, "tensor"),
    )
    out_specs = (
        P("dp", None, "tensor"),
        P("dp", "tensor", None),
        P("dp", None, "tensor"),
        P(),
        P(),
        P("tensor"),
        P("tensor"),
    )
    return jax.shard_map(body, mesh=mesh, in_specs=in_specs, out_specs=out_specs, check_vma=False)
```

```python
import functools
import math

import jax
import jax.numpy as jnp
from jax import lax
from jax.experimental import pallas as pl
from jax.experimental.pallas import tpu as pltpu
from jax.sharding import PartitionSpec as P

HDIM = 128
BLK = 128
EPS = 1e-06
AXES = ("dp", "tensor")
N_DP = 8
N_T = 16
VMEM_LIMIT = 22 * 1024 * 1024
TINY = pl.CostEstimate(flops=1000, bytes_accessed=1000, transcendentals=0)
F32 = jnp.float32
BF16 = jnp.bfloat16


def ring_pairs(ring, flip):
    pairs = []
    for dp in range(N_DP):
        for t in range(N_T):
            along_x = (dp % 2 == 0) == (ring == 1)
            pairs.append((dp * N_T + t, dp * N_T + (t ^ (flip if along_x else 4 * flip))))
    return pairs


def swap(value, ring, flip):
    return lax.ppermute(value, AXES, ring_pairs(ring, flip))


def across(value, flip):
    return lax.ppermute(value, "dp", [(k, k ^ flip) for k in range(N_DP)])


def add(*parts):
    return sum(p.astype(F32) for p in parts).astype(BF16)


def add_rows(value, more, start):
    rows = more.shape[0]
    return lax.dynamic_update_slice(value, add(value[start : start + rows], more), (start, 0))


def centre(wide):
    centred = wide - jnp.mean(wide, axis=-1, keepdims=True)
    factor = lax.rsqrt(jnp.mean(centred * centred, axis=-1, keepdims=True) + EPS)
    return centred * factor, factor


def norm_kernel(x_ref, gain_ref, bias_ref, out_ref):
    hat, _ = centre(x_ref[...].astype(F32))
    out_ref[...] = (hat * gain_ref[...] + bias_ref[...]).astype(BF16)


def norm_rows(x, gain, bias):
    return pl.pallas_call(
        norm_kernel,
        out_shape=jax.ShapeDtypeStruct(x.shape, BF16),
        compiler_params=pltpu.CompilerParams(vmem_limit_bytes=VMEM_LIMIT),
        cost_estimate=TINY,
        name="norm_rows",
    )(x, gain, bias)


def patch_kernel(x_ref, gain_ref, own_ref, got1_ref, got3_ref, out_ref):
    hat, factor = centre(x_ref[...].astype(F32))
    grad = own_ref[0:BLK].astype(F32) + got1_ref[...].astype(F32) + got3_ref[...].astype(F32)
    scaled = grad * gain_ref[...]
    out_ref[...] = (
        factor
        * (
            scaled
            - jnp.mean(scaled, axis=-1, keepdims=True)
            - hat * jnp.mean(scaled * hat, axis=-1, keepdims=True)
        )
    ).astype(BF16)


def patch_rows(x, gain, *pieces):
    return pl.pallas_call(
        patch_kernel,
        out_shape=jax.ShapeDtypeStruct(x.shape, BF16),
        compiler_params=pltpu.CompilerParams(vmem_limit_bytes=VMEM_LIMIT),
        cost_estimate=TINY,
        name="patch_rows",
    )(x, gain, *pieces)


def shard_labels(counts_ref, shard, shape, dim):
    first = (shard // 2) * 2
    merged = counts_ref[first] > BLK
    image = jnp.where(merged, first, shard)
    count = counts_ref[image]
    offset = lax.broadcasted_iota(jnp.int32, shape, dim) + BLK * (shard - image)
    return jnp.where(offset < count, image, -1 - shard)


def whole(w_ref):
    return jnp.concatenate([w_ref[part] for part in range(3)], axis=1)


def nt(left, right):
    return lax.dot_general(left, right, (((1,), (1,)), ((), ())), preferred_element_type=F32)


def tn(left, right):
    return lax.dot_general(left, right, (((0,), (0,)), ((), ())), preferred_element_type=F32)


def back(grad, hat, factor, gain):
    scaled = grad * gain
    return factor * (
        scaled
        - jnp.mean(scaled, axis=-1, keepdims=True)
        - hat * jnp.mean(scaled * hat, axis=-1, keepdims=True)
    )


def quad_kernel(n_slots, n_outs, first, meta, counts, *refs):
    refs = list(refs)
    slots = [refs.pop(0) for _ in range(n_slots)]
    w_ref, up_ref, qg_ref, kg_ref = [refs.pop(0) for _ in range(4)]
    if not first:
        norms_in, terms_in, _ = [refs.pop(0) for _ in range(3)]
    att_ref = refs.pop(0)
    dnormed = [refs.pop(0) for _ in range(n_outs)]
    dproj_ref, norms_ref, terms_ref, proj, dbuf, abuf, sems = refs
    core = meta[0]
    places = [0, 1 + core, 2 - core, 3]

    def rows_of(place):
        return pl.ds(pl.multiple_of(place * BLK, BLK), BLK)

    def taken(refs, side):
        start = 0
        found = []
        for ref in refs:
            if start // (2 * BLK) == side:
                found.append((ref, start % (2 * BLK)))
            start += ref.shape[0]
        return found

    def rows_in(side):
        return jnp.concatenate([ref[...] for ref, _ in taken(slots, side)], axis=0)

    for side in range(2):
        result = jnp.dot(rows_in(side), whole(w_ref), preferred_element_type=F32)
        for k in range(2):
            proj[rows_of(places[2 * side + k]), :] = result[k * BLK : (k + 1) * BLK]

    scale = 1.0 / math.sqrt(HDIM)
    q_terms = [None, None]
    k_terms = [None, None]
    copies = []
    for pair in range(2):
        shards = [meta[1 + 2 * pair + k] for k in range(2)]
        columns = jnp.concatenate([shard_labels(counts, s, (BLK, 1), 0) for s in shards], axis=0)
        across = jnp.concatenate([shard_labels(counts, s, (1, BLK), 1) for s in shards], axis=1)
        same = columns == across
        rows = slice(pair * 2 * BLK, (pair + 1) * 2 * BLK)
        for head in range(2):
            cols = slice(head * HDIM, (head + 1) * HDIM)
            q_gain = qg_ref[:, cols]
            k_gain = kg_ref[:, cols]
            q_hat, q_factor = centre(proj[rows, head * HDIM : (head + 1) * HDIM])
            k_hat, k_factor = centre(proj[rows, (2 + head) * HDIM : (3 + head) * HDIM])
            value = proj[rows, (4 + head) * HDIM : (5 + head) * HDIM].astype(BF16)
            q_s = (q_hat * q_gain).astype(BF16)
            k_s = (k_hat * k_gain).astype(BF16)
            grad = jnp.concatenate([up_ref[rows_of(s), cols] for s in shards], axis=0)
            weights = jnp.where(same, jnp.exp(nt(q_s, k_s) * scale), 0.0)
            probs = weights * (1.0 / jnp.sum(weights, axis=-1, keepdims=True))
            probs_b = probs.astype(BF16)
            abuf[rows, cols] = jnp.dot(probs_b, value, preferred_element_type=F32).astype(BF16)
            dprob = nt(grad, value)
            inner = jnp.sum(probs * dprob, axis=-1, keepdims=True)
            dscore = (probs * (dprob - inner) * scale).astype(BF16)
            dvalue = tn(probs_b, grad)
            dquery = jnp.dot(dscore, k_s, preferred_element_type=F32)
            dkey = tn(dscore, q_s)
            q_term = jnp.sum(dquery * q_hat, axis=0, keepdims=True)
            k_term = jnp.sum(dkey * k_hat, axis=0, keepdims=True)
            q_terms[head] = q_term if pair == 0 else q_terms[head] + q_term
            k_terms[head] = k_term if pair == 0 else k_terms[head] + k_term
            dbuf[rows, head * HDIM : (head + 1) * HDIM] = back(dquery, q_hat, q_factor, q_gain).astype(BF16)
            dbuf[rows, (2 + head) * HDIM : (3 + head) * HDIM] = back(dkey, k_hat, k_factor, k_gain).astype(BF16)
            dbuf[rows, (4 + head) * HDIM : (5 + head) * HDIM] = dvalue.astype(BF16)
        for k in range(2):
            place = 2 * pair + k
            copy = pltpu.make_async_copy(
                abuf.at[pl.ds(place * BLK, BLK)], att_ref.at[rows_of(shards[k])], sems.at[place]
            )
            copy.start()
            copies.append(copy)
    terms = jnp.concatenate(q_terms + k_terms, axis=1)
    terms_ref[...] = terms if first else terms_in[...] + terms

    for side in range(2):
        part = jnp.concatenate([dbuf[rows_of(places[2 * side + k]), :] for k in range(2)], axis=0)
        dproj_ref[side * 2 * BLK : (side + 1) * 2 * BLK] = part
        result = nt(part, whole(w_ref))
        sums = jnp.concatenate(
            [
                jnp.sum(result * rows_in(side).astype(F32), axis=0, keepdims=True),
                jnp.sum(result, axis=0, keepdims=True),
            ],
            axis=1,
        )
        if side == 0:
            norms_ref[...] = sums if first else norms_in[...] + sums
        else:
            norms_ref[...] += sums
        for ref, start in taken(dnormed, side):
            ref[...] = result[start : start + ref.shape[0]].astype(BF16)
    for copy in copies:
        copy.wait()


def quad(meta, counts, slots, outs, weight, upstream, q_gain, k_gain, before):
    length, heads = upstream.shape
    width = weight.shape[1]
    cols = 3 * heads
    first = before is None
    vmem = pl.BlockSpec(memory_space=pltpu.VMEM)
    smem = pl.BlockSpec(memory_space=pltpu.SMEM)
    anywhere = pl.BlockSpec(memory_space=pl.ANY)
    operands = [meta, counts, *slots, weight, upstream, q_gain, k_gain]
    in_specs = [smem, smem] + [vmem] * (len(operands) - 2)
    aliases = {}
    if not first:
        operands += before
        in_specs += [vmem, vmem, anywhere]
        aliases = {len(operands) - 1: 0}
    found = pl.pallas_call(
        functools.partial(quad_kernel, len(slots), len(outs), first),
        in_specs=in_specs,
        out_specs=[anywhere] + [vmem] * (len(outs) + 3),
        out_shape=[jax.ShapeDtypeStruct((length, heads), BF16)]
        + [jax.ShapeDtypeStruct((rows, width), BF16) for rows in outs]
        + [
            jax.ShapeDtypeStruct((4 * BLK, cols), BF16),
            jax.ShapeDtypeStruct((1, 2 * width), F32),
            jax.ShapeDtypeStruct((1, 2 * heads), F32),
        ],
        scratch_shapes=[
            pltpu.VMEM((4 * BLK, cols), F32),
            pltpu.VMEM((4 * BLK, cols), BF16),
            pltpu.VMEM((4 * BLK, heads), BF16),
            pltpu.SemaphoreType.DMA((4,)),
        ],
        input_output_aliases=aliases,
        compiler_params=pltpu.CompilerParams(vmem_limit_bytes=VMEM_LIMIT),
        cost_estimate=TINY,
        name="quad",
    )(*operands)
    attention, *dnormed, dproj, norms, terms = found
    return [norms, terms, attention], dnormed, dproj


def weight_kernel(n_rows, place, *refs):
    rows = refs[:n_rows]
    dprojs = refs[n_rows : n_rows + 4]
    out_ref = refs[-1]
    left = jnp.concatenate([ref[...] for ref in rows], axis=0)
    right = jnp.concatenate([ref[...] for ref in dprojs], axis=0)
    out_ref[...] = tn(left, right).astype(BF16)


def weight_grads(dp, rows, dprojs, odd):
    width = rows[0].shape[1]
    cols = dprojs[0].shape[1]
    tile = width // N_DP
    steps = N_DP // 2
    return pl.pallas_call(
        functools.partial(weight_kernel, len(rows)),
        grid_spec=pltpu.PrefetchScalarGridSpec(
            num_scalar_prefetch=1,
            grid=(steps,),
            in_specs=[
                pl.BlockSpec((r.shape[0], tile), lambda i, place: (0, place[0] ^ (2 * i + odd))) for r in rows
            ]
            + [pl.BlockSpec(d.shape, lambda i, place: (0, 0)) for d in dprojs],
            out_specs=pl.BlockSpec((tile, cols), lambda i, place: (i, 0)),
        ),
        out_shape=jax.ShapeDtypeStruct((steps * tile, cols), BF16),
        compiler_params=pltpu.CompilerParams(vmem_limit_bytes=VMEM_LIMIT),
        cost_estimate=TINY,
        name="weight_grads",
    )(dp, *rows, *dprojs)


def share_kernel(factor, own_ref, got1_ref, got3_ref, out_ref):
    cols = out_ref.shape[2]
    total = own_ref[0 : got1_ref.shape[0]].astype(F32) + got1_ref[...].astype(F32)
    total = (total + got3_ref[...].astype(F32)) * factor
    for part in range(3):
        out_ref[part] = total[:, part * cols : (part + 1) * cols]


def weight_out(own, got1, got3, factor):
    rows, cols = got1.shape
    return pl.pallas_call(
        functools.partial(share_kernel, factor),
        out_shape=jax.ShapeDtypeStruct((3, rows, cols // 3), F32),
        compiler_params=pltpu.CompilerParams(vmem_limit_bytes=VMEM_LIMIT),
        cost_estimate=TINY,
        name="weight_out",
    )(own, got1, got3).transpose(1, 0, 2)


def quad_meta(core, tensor, i, j):
    found = [core]
    for place in range(4):
        straight = (i + place // 2) * 4 + j + place % 2
        turned = (j + place // 2) * 4 + i + place % 2
        found.append(tensor ^ jnp.where(core == 0, straight, turned))
    return jnp.stack(found).astype(jnp.int32)


def total_over(value, axis, flips):
    size = lax.axis_size(axis)
    for flip in flips:
        value = value + lax.ppermute(value, axis, [(k, k ^ flip) for k in range(size)])
    return value


def together(*values):
    return lax.optimization_barrier(values)


def together(*values):
    return lax.optimization_barrier(values)


def body(patches, counts, norm_gain, norm_bias, qkv_weight, query_gain, key_gain, upstream):
    width = patches.shape[2]
    local = qkv_weight.shape[2]
    length = upstream.shape[1]
    factor = 1.0 / math.sqrt(lax.axis_size("dp") * length)
    dp = lax.axis_index("dp")
    core = dp % 2
    tensor = lax.axis_index("tensor")
    gain = norm_gain.reshape(1, width)
    bias = norm_bias.reshape(1, width)
    weight = qkv_weight.transpose(1, 0, 2)
    own_rows = patches[0]
    half = BLK // 2

    own = norm_rows(own_rows, gain, bias)
    near, next3 = swap(own, 1, 1), swap(own, 1, 3)
    metas = [quad_meta(core, tensor, i, j) for i, j in ((0, 0), (2, 0), (0, 2), (2, 2))]
    near, next3, *metas = together(near, next3, *metas)
    top, bottom = swap(next3[:half], 1, 1), swap(near[half:], 1, 3)
    a0 = jnp.concatenate([own, near], axis=0)
    a1, a3 = swap(a0, 2, 1), swap(a0, 2, 3)
    b0 = jnp.concatenate([top, bottom, next3], axis=0)
    b1, b3 = swap(b0, 2, 1), swap(b0, 2, 3)
    a2_top, a2_bottom = swap(a3[:BLK], 2, 1), swap(a1[BLK:], 2, 3)

    def run(meta, slots, outs, before):
        return quad(
            meta,
            counts[0],
            slots,
            outs,
            weight,
            upstream[0],
            query_gain.reshape(1, local),
            key_gain.reshape(1, local),
            before,
        )

    near_outs, far_outs = [2 * BLK, 2 * BLK], [BLK, BLK, 2 * BLK]
    state, (da0, da1), dproj0 = run(metas[0], [a0, a1], near_outs, None)
    state[0], b1, b3 = together(state[0], b1, b3)
    b2_top, b2_bottom = swap(b3[:BLK], 2, 1), swap(b1[BLK:], 2, 3)
    state, (db0, db1), dproj2 = run(metas[2], [b0, b1], near_outs, state)
    state[0], a2_top, a2_bottom, a3 = together(state[0], a2_top, a2_bottom, a3)
    state, (da2_top, da2_bottom, da3), dproj1 = run(metas[1], [a2_top, a2_bottom, a3], far_outs, state)
    fa_top, fa_bottom = swap(da2_top, 2, 3), swap(da2_bottom, 2, 1)
    state[0], b2_top, b2_bottom = together(state[0], b2_top, b2_bottom)
    state, (db2_top, db2_bottom, db3), dproj3 = run(metas[3], [b2_top, b2_bottom, b3], far_outs, state)
    norms, terms, attention = state

    norms, fa_top, fa_bottom = together(norms, fa_top, fa_bottom)
    da1, da3 = add_rows(da1, fa_top, 0), add_rows(da3, fa_bottom, BLK)
    norms, da1, da3, db2_top, db2_bottom, dproj3 = together(norms, da1, da3, db2_top, db2_bottom, dproj3)
    fb_top, fb_bottom = swap(db2_top, 2, 3), swap(db2_bottom, 2, 1)
    ga1, ga3 = swap(da1, 2, 1), swap(da3, 2, 3)
    rows = [a0, a1, b0, b1, a2_top, a2_bottom, a3, b2_top, b2_bottom, b3]
    place = dp.astype(jnp.int32).reshape(1)
    dprojs = [dproj0, dproj2, dproj1, dproj3]
    other = weight_grads(place, rows, dprojs, 1)
    mine = weight_grads(place, rows, dprojs, 0)
    small = total_over(jnp.concatenate([norms, terms], axis=1), "dp", (1, 2))
    other, mine, small, fb_top, fb_bottom, ga1, ga3 = together(
        other, mine, small, fb_top, fb_bottom, ga1, ga3
    )

    db1, db3 = add_rows(db1, fb_top, 0), add_rows(db3, fb_bottom, BLK)
    db1, db3, other, mine, small = together(db1, db3, other, mine, small)
    gb1, gb3 = swap(db1, 2, 1), swap(db3, 2, 3)
    from_core = across(other, 1)
    small = total_over(small, "dp", (4,))
    small, terms = small[:, : 2 * width], small[:, 2 * width :]
    small = total_over(small, "tensor", (1,))
    r_near = add(da0, ga1, ga3)
    both = add(mine, from_core)
    share = both.shape[0] // 4
    cut = share // 2
    y_top, y_bottom = across(both[2 * share : 2 * share + cut], 6), across(both[2 * share + cut : 3 * share], 2)
    y_top, y_bottom, small, gb1, gb3, r_near = together(y_top, y_bottom, small, gb1, gb3, r_near)

    r_far = add(db0, gb1, gb3)
    y1 = add_rows(both[share : 2 * share], y_top, 0)
    y3 = add_rows(both[3 * share :], y_bottom, cut)
    r_far, y1, y3, small = together(r_far, y1, y3, small)
    u_top, u_bottom = swap(r_far[:half], 1, 3), swap(r_far[half:BLK], 1, 1)
    z1, z3 = across(y1, 2), across(y3, 6)
    small = total_over(small, "tensor", (2,))
    small, u_top, u_bottom = together(small, u_top, u_bottom)
    v1, v3 = add_rows(r_near[BLK:], u_top, 0), add_rows(r_far[BLK:], u_bottom, half)
    small, v1, v3 = together(small, v1, v3)
    v1, v3 = swap(v1, 1, 1), swap(v3, 1, 3)
    small = total_over(small, "tensor", (4,))
    small, v1, v3, z1, z3 = together(small, v1, v3, z1, z3)
    small = total_over(small, "tensor", (8,)) * factor
    weight_grad = weight_out(both, z1, z3, factor)
    patch_grad = patch_rows(own_rows, gain, r_near, v1, v3)
    shift = small[:, width : 2 * width]
    gain_grad = (small[:, :width] - bias * shift) / gain
    return (
        attention.reshape(1, length, local),
        patch_grad[None],
        weight_grad,
        gain_grad[0],
        shift[0],
        terms[0, :local] * factor,
        terms[0, local:] * factor,
    )


def solution(mesh):
    in_specs = (
        P("dp", "tensor", None),
        P("dp", None),
        P(),
        P(),
        P(None, None, "tensor"),
        P("tensor"),
        P("tensor"),
        P("dp", None, "tensor"),
    )
    out_specs = (
        P("dp", None, "tensor"),
        P("dp", "tensor", None),
        P("dp", None, "tensor"),
        P(),
        P(),
        P("tensor"),
        P("tensor"),
    )
    return jax.shard_map(body, mesh=mesh, in_specs=in_specs, out_specs=out_specs, check_vma=False)
```

```python
import functools
import math

import jax
import jax.numpy as jnp
from jax import lax
from jax.experimental import pallas as pl
from jax.experimental.pallas import tpu as pltpu
from jax.sharding import PartitionSpec as P

HDIM = 128
BLK = 128
EPS = 1e-06
AXES = ("dp", "tensor")
N_DP = 8
N_T = 16
VMEM_LIMIT = 22 * 1024 * 1024
TINY = pl.CostEstimate(flops=1000, bytes_accessed=1000, transcendentals=0)
F32 = jnp.float32
BF16 = jnp.bfloat16


def ring_pairs(ring, flip):
    pairs = []
    for dp in range(N_DP):
        for t in range(N_T):
            along_x = (dp % 2 == 0) == (ring == 1)
            pairs.append((dp * N_T + t, dp * N_T + (t ^ (flip if along_x else 4 * flip))))
    return pairs


def swap(value, ring, flip):
    return lax.ppermute(value, AXES, ring_pairs(ring, flip))


def across(value, flip):
    return lax.ppermute(value, "dp", [(k, k ^ flip) for k in range(N_DP)])


def add(*parts):
    return sum(p.astype(F32) for p in parts).astype(BF16)


def add_rows(value, more, start):
    rows = more.shape[0]
    return lax.dynamic_update_slice(value, add(value[start : start + rows], more), (start, 0))


def centre(wide):
    centred = wide - jnp.mean(wide, axis=-1, keepdims=True)
    factor = lax.rsqrt(jnp.mean(centred * centred, axis=-1, keepdims=True) + EPS)
    return centred * factor, factor


def norm_kernel(x_ref, gain_ref, bias_ref, out_ref):
    hat, _ = centre(x_ref[...].astype(F32))
    out_ref[...] = (hat * gain_ref[...] + bias_ref[...]).astype(BF16)


def norm_rows(x, gain, bias):
    return pl.pallas_call(
        norm_kernel,
        out_shape=jax.ShapeDtypeStruct(x.shape, BF16),
        compiler_params=pltpu.CompilerParams(vmem_limit_bytes=VMEM_LIMIT),
        cost_estimate=TINY,
        name="norm_rows",
    )(x, gain, bias)


def patch_kernel(x_ref, gain_ref, own_ref, got1_ref, got3_ref, out_ref):
    hat, factor = centre(x_ref[...].astype(F32))
    grad = own_ref[0:BLK].astype(F32) + got1_ref[...].astype(F32) + got3_ref[...].astype(F32)
    scaled = grad * gain_ref[...]
    out_ref[...] = (
        factor
        * (
            scaled
            - jnp.mean(scaled, axis=-1, keepdims=True)
            - hat * jnp.mean(scaled * hat, axis=-1, keepdims=True)
        )
    ).astype(BF16)


def patch_rows(x, gain, *pieces):
    return pl.pallas_call(
        patch_kernel,
        out_shape=jax.ShapeDtypeStruct(x.shape, BF16),
        compiler_params=pltpu.CompilerParams(vmem_limit_bytes=VMEM_LIMIT),
        cost_estimate=TINY,
        name="patch_rows",
    )(x, gain, *pieces)


def shard_labels(counts_ref, shard, shape, dim):
    first = (shard // 2) * 2
    merged = counts_ref[first] > BLK
    image = jnp.where(merged, first, shard)
    count = counts_ref[image]
    offset = lax.broadcasted_iota(jnp.int32, shape, dim) + BLK * (shard - image)
    return jnp.where(offset < count, image, -1 - shard)


def whole(w_ref):
    return jnp.concatenate([w_ref[part] for part in range(3)], axis=1)


def nt(left, right):
    return lax.dot_general(left, right, (((1,), (1,)), ((), ())), preferred_element_type=F32)


def tn(left, right):
    return lax.dot_general(left, right, (((0,), (0,)), ((), ())), preferred_element_type=F32)


def back(grad, hat, factor, gain):
    scaled = grad * gain
    return factor * (
        scaled
        - jnp.mean(scaled, axis=-1, keepdims=True)
        - hat * jnp.mean(scaled * hat, axis=-1, keepdims=True)
    )


def quad_kernel(n_slots, n_outs, first, meta, counts, *refs):
    refs = list(refs)
    slots = [refs.pop(0) for _ in range(n_slots)]
    w_ref, up_ref, qg_ref, kg_ref = [refs.pop(0) for _ in range(4)]
    if not first:
        norms_in, terms_in, _ = [refs.pop(0) for _ in range(3)]
    att_ref = refs.pop(0)
    dnormed = [refs.pop(0) for _ in range(n_outs)]
    dproj_ref, norms_ref, terms_ref, proj, dbuf, abuf, sems = refs
    core = meta[0]
    places = [0, 1 + core, 2 - core, 3]

    def rows_of(place):
        return pl.ds(pl.multiple_of(place * BLK, BLK), BLK)

    def taken(refs, side):
        start = 0
        found = []
        for ref in refs:
            if start // (2 * BLK) == side:
                found.append((ref, start % (2 * BLK)))
            start += ref.shape[0]
        return found

    def rows_in(side):
        return jnp.concatenate([ref[...] for ref, _ in taken(slots, side)], axis=0)

    for side in range(2):
        result = jnp.dot(rows_in(side), whole(w_ref), preferred_element_type=F32)
        for k in range(2):
            proj[rows_of(places[2 * side + k]), :] = result[k * BLK : (k + 1) * BLK]

    scale = 1.0 / math.sqrt(HDIM)
    q_terms = [None, None]
    k_terms = [None, None]
    copies = []
    for pair in range(2):
        shards = [meta[1 + 2 * pair + k] for k in range(2)]
        columns = jnp.concatenate([shard_labels(counts, s, (BLK, 1), 0) for s in shards], axis=0)
        across = jnp.concatenate([shard_labels(counts, s, (1, BLK), 1) for s in shards], axis=1)
        same = columns == across
        rows = slice(pair * 2 * BLK, (pair + 1) * 2 * BLK)
        for head in range(2):
            cols = slice(head * HDIM, (head + 1) * HDIM)
            q_gain = qg_ref[:, cols]
            k_gain = kg_ref[:, cols]
            q_hat, q_factor = centre(proj[rows, head * HDIM : (head + 1) * HDIM])
            k_hat, k_factor = centre(proj[rows, (2 + head) * HDIM : (3 + head) * HDIM])
            value = proj[rows, (4 + head) * HDIM : (5 + head) * HDIM].astype(BF16)
            q_s = (q_hat * q_gain).astype(BF16)
            k_s = (k_hat * k_gain).astype(BF16)
            grad = jnp.concatenate([up_ref[rows_of(s), cols] for s in shards], axis=0)
            weights = jnp.where(same, jnp.exp(nt(q_s, k_s) * scale), 0.0)
            probs = weights * (1.0 / jnp.sum(weights, axis=-1, keepdims=True))
            probs_b = probs.astype(BF16)
            abuf[rows, cols] = jnp.dot(probs_b, value, preferred_element_type=F32).astype(BF16)
            dprob = nt(grad, value)
            inner = jnp.sum(probs * dprob, axis=-1, keepdims=True)
            dscore = (probs * (dprob - inner) * scale).astype(BF16)
            dvalue = tn(probs_b, grad)
            dquery = jnp.dot(dscore, k_s, preferred_element_type=F32)
            dkey = tn(dscore, q_s)
            q_term = jnp.sum(dquery * q_hat, axis=0, keepdims=True)
            k_term = jnp.sum(dkey * k_hat, axis=0, keepdims=True)
            q_terms[head] = q_term if pair == 0 else q_terms[head] + q_term
            k_terms[head] = k_term if pair == 0 else k_terms[head] + k_term
            dbuf[rows, head * HDIM : (head + 1) * HDIM] = back(dquery, q_hat, q_factor, q_gain).astype(BF16)
            dbuf[rows, (2 + head) * HDIM : (3 + head) * HDIM] = back(dkey, k_hat, k_factor, k_gain).astype(BF16)
            dbuf[rows, (4 + head) * HDIM : (5 + head) * HDIM] = dvalue.astype(BF16)
        for k in range(2):
            place = 2 * pair + k
            copy = pltpu.make_async_copy(
                abuf.at[pl.ds(place * BLK, BLK)], att_ref.at[rows_of(shards[k])], sems.at[place]
            )
            copy.start()
            copies.append(copy)
    terms = jnp.concatenate(q_terms + k_terms, axis=1)
    terms_ref[...] = terms if first else terms_in[...] + terms

    for side in range(2):
        part = jnp.concatenate([dbuf[rows_of(places[2 * side + k]), :] for k in range(2)], axis=0)
        dproj_ref[side * 2 * BLK : (side + 1) * 2 * BLK] = part
        result = nt(part, whole(w_ref))
        sums = jnp.concatenate(
            [
                jnp.sum(result * rows_in(side).astype(F32), axis=0, keepdims=True),
                jnp.sum(result, axis=0, keepdims=True),
            ],
            axis=1,
        )
        if side == 0:
            norms_ref[...] = sums if first else norms_in[...] + sums
        else:
            norms_ref[...] += sums
        for ref, start in taken(dnormed, side):
            ref[...] = result[start : start + ref.shape[0]].astype(BF16)
    for copy in copies:
        copy.wait()


def quad(meta, counts, slots, outs, weight, upstream, q_gain, k_gain, before):
    length, heads = upstream.shape
    width = weight.shape[1]
    cols = 3 * heads
    first = before is None
    vmem = pl.BlockSpec(memory_space=pltpu.VMEM)
    smem = pl.BlockSpec(memory_space=pltpu.SMEM)
    anywhere = pl.BlockSpec(memory_space=pl.ANY)
    operands = [meta, counts, *slots, weight, upstream, q_gain, k_gain]
    in_specs = [smem, smem] + [vmem] * (len(operands) - 2)
    aliases = {}
    if not first:
        operands += before
        in_specs += [vmem, vmem, anywhere]
        aliases = {len(operands) - 1: 0}
    found = pl.pallas_call(
        functools.partial(quad_kernel, len(slots), len(outs), first),
        in_specs=in_specs,
        out_specs=[anywhere] + [vmem] * (len(outs) + 3),
        out_shape=[jax.ShapeDtypeStruct((length, heads), BF16)]
        + [jax.ShapeDtypeStruct((rows, width), BF16) for rows in outs]
        + [
            jax.ShapeDtypeStruct((4 * BLK, cols), BF16),
            jax.ShapeDtypeStruct((1, 2 * width), F32),
            jax.ShapeDtypeStruct((1, 2 * heads), F32),
        ],
        scratch_shapes=[
            pltpu.VMEM((4 * BLK, cols), F32),
            pltpu.VMEM((4 * BLK, cols), BF16),
            pltpu.VMEM((4 * BLK, heads), BF16),
            pltpu.SemaphoreType.DMA((4,)),
        ],
        input_output_aliases=aliases,
        compiler_params=pltpu.CompilerParams(vmem_limit_bytes=VMEM_LIMIT),
        cost_estimate=TINY,
        name="quad",
    )(*operands)
    attention, *dnormed, dproj, norms, terms = found
    return [norms, terms, attention], dnormed, dproj


def weight_kernel(n_rows, place, *refs):
    rows = refs[:n_rows]
    dprojs = refs[n_rows : n_rows + 4]
    out_ref = refs[-1]
    left = jnp.concatenate([ref[...] for ref in rows], axis=0)
    right = jnp.concatenate([ref[...] for ref in dprojs], axis=0)
    out_ref[...] = tn(left, right).astype(BF16)


def weight_grads(dp, rows, dprojs, odd):
    width = rows[0].shape[1]
    cols = dprojs[0].shape[1]
    tile = width // N_DP
    steps = N_DP // 2
    return pl.pallas_call(
        functools.partial(weight_kernel, len(rows)),
        grid_spec=pltpu.PrefetchScalarGridSpec(
            num_scalar_prefetch=1,
            grid=(steps,),
            in_specs=[
                pl.BlockSpec((r.shape[0], tile), lambda i, place: (0, place[0] ^ (2 * i + odd))) for r in rows
            ]
            + [pl.BlockSpec(d.shape, lambda i, place: (0, 0)) for d in dprojs],
            out_specs=pl.BlockSpec((tile, cols), lambda i, place: (i, 0)),
        ),
        out_shape=jax.ShapeDtypeStruct((steps * tile, cols), BF16),
        compiler_params=pltpu.CompilerParams(vmem_limit_bytes=VMEM_LIMIT),
        cost_estimate=TINY,
        name="weight_grads",
    )(dp, *rows, *dprojs)


def share_kernel(factor, own_ref, got1_ref, got3_ref, out_ref):
    cols = out_ref.shape[2]
    total = own_ref[0 : got1_ref.shape[0]].astype(F32) + got1_ref[...].astype(F32)
    total = (total + got3_ref[...].astype(F32)) * factor
    for part in range(3):
        out_ref[part] = total[:, part * cols : (part + 1) * cols]


def weight_out(own, got1, got3, factor):
    rows, cols = got1.shape
    return pl.pallas_call(
        functools.partial(share_kernel, factor),
        out_shape=jax.ShapeDtypeStruct((3, rows, cols // 3), F32),
        compiler_params=pltpu.CompilerParams(vmem_limit_bytes=VMEM_LIMIT),
        cost_estimate=TINY,
        name="weight_out",
    )(own, got1, got3).transpose(1, 0, 2)


def quad_meta(core, tensor, i, j):
    found = [core]
    for place in range(4):
        straight = (i + place // 2) * 4 + j + place % 2
        turned = (j + place // 2) * 4 + i + place % 2
        found.append(tensor ^ jnp.where(core == 0, straight, turned))
    return jnp.stack(found).astype(jnp.int32)


def total_over(value, axis, flips):
    size = lax.axis_size(axis)
    for flip in flips:
        value = value + lax.ppermute(value, axis, [(k, k ^ flip) for k in range(size)])
    return value


def together(*values):
    return lax.optimization_barrier(values)


def together(*values):
    return lax.optimization_barrier(values)


def body(patches, counts, norm_gain, norm_bias, qkv_weight, query_gain, key_gain, upstream):
    width = patches.shape[2]
    local = qkv_weight.shape[2]
    length = upstream.shape[1]
    factor = 1.0 / math.sqrt(lax.axis_size("dp") * length)
    dp = lax.axis_index("dp")
    core = dp % 2
    tensor = lax.axis_index("tensor")
    gain = norm_gain.reshape(1, width)
    bias = norm_bias.reshape(1, width)
    weight = qkv_weight.transpose(1, 0, 2)
    own_rows = patches[0]
    half = BLK // 2

    own = norm_rows(own_rows, gain, bias)
    near, next3 = swap(own, 1, 1), swap(own, 1, 3)
    metas = [quad_meta(core, tensor, i, j) for i, j in ((0, 0), (2, 0), (0, 2), (2, 2))]
    near, next3, *metas = together(near, next3, *metas)
    top, bottom = swap(next3[:half], 1, 1), swap(near[half:], 1, 3)
    a0 = jnp.concatenate([own, near], axis=0)
    a1, a3 = swap(a0, 2, 1), swap(a0, 2, 3)
    b0 = jnp.concatenate([top, bottom, next3], axis=0)
    b1, b3 = swap(b0, 2, 1), swap(b0, 2, 3)
    a2_top, a2_bottom = swap(a3[:BLK], 2, 1), swap(a1[BLK:], 2, 3)

    def run(meta, slots, outs, before):
        return quad(
            meta,
            counts[0],
            slots,
            outs,
            weight,
            upstream[0],
            query_gain.reshape(1, local),
            key_gain.reshape(1, local),
            before,
        )

    near_outs, far_outs = [2 * BLK, 2 * BLK], [BLK, BLK, 2 * BLK]
    state, (da0, da1), dproj0 = run(metas[0], [a0, a1], near_outs, None)
    state[0], b1, b3 = together(state[0], b1, b3)
    b2_top, b2_bottom = swap(b3[:BLK], 2, 1), swap(b1[BLK:], 2, 3)
    state, (db0, db1), dproj2 = run(metas[2], [b0, b1], near_outs, state)
    state[0], a2_top, a2_bottom, a3 = together(state[0], a2_top, a2_bottom, a3)
    state, (da2_top, da2_bottom, da3), dproj1 = run(metas[1], [a2_top, a2_bottom, a3], far_outs, state)
    fa_top, fa_bottom = swap(da2_top, 2, 3), swap(da2_bottom, 2, 1)
    state[0], b2_top, b2_bottom = together(state[0], b2_top, b2_bottom)
    state, (db2_top, db2_bottom, db3), dproj3 = run(metas[3], [b2_top, b2_bottom, b3], far_outs, state)
    norms, terms, attention = state

    norms, fa_top, fa_bottom = together(norms, fa_top, fa_bottom)
    da1, da3 = add_rows(da1, fa_top, 0), add_rows(da3, fa_bottom, BLK)
    norms, da1, da3, db2_top, db2_bottom, dproj3 = together(norms, da1, da3, db2_top, db2_bottom, dproj3)
    fb_top, fb_bottom = swap(db2_top, 2, 3), swap(db2_bottom, 2, 1)
    ga1, ga3 = swap(da1, 2, 1), swap(da3, 2, 3)
    rows = [a0, a1, b0, b1, a2_top, a2_bottom, a3, b2_top, b2_bottom, b3]
    place = dp.astype(jnp.int32).reshape(1)
    dprojs = [dproj0, dproj2, dproj1, dproj3]
    other = weight_grads(place, rows, dprojs, 1)
    mine = weight_grads(place, rows, dprojs, 0)
    small = total_over(jnp.concatenate([norms, terms], axis=1), "dp", (1, 2))
    other, mine, small, fb_top, fb_bottom, ga1, ga3 = together(
        other, mine, small, fb_top, fb_bottom, ga1, ga3
    )

    db1, db3 = add_rows(db1, fb_top, 0), add_rows(db3, fb_bottom, BLK)
    db1, db3, other, mine, small = together(db1, db3, other, mine, small)
    gb1, gb3 = swap(db1, 2, 1), swap(db3, 2, 3)
    from_core = across(other, 1)
    small = total_over(small, "dp", (4,))
    small, terms = small[:, : 2 * width], small[:, 2 * width :]
    small = total_over(small, "tensor", (1,))
    r_near = add(da0, ga1, ga3)
    both = add(mine, from_core)
    share = both.shape[0] // 4
    cut = share // 2
    y_top, y_bottom = across(both[2 * share : 2 * share + cut], 6), across(both[2 * share + cut : 3 * share], 2)
    y_top, y_bottom, small, gb1, gb3, r_near = together(y_top, y_bottom, small, gb1, gb3, r_near)

    r_far = add(db0, gb1, gb3)
    y1 = add_rows(both[share : 2 * share], y_top, 0)
    y3 = add_rows(both[3 * share :], y_bottom, cut)
    r_far, y1, y3, small = together(r_far, y1, y3, small)
    u_top, u_bottom = swap(r_far[:half], 1, 3), swap(r_far[half:BLK], 1, 1)
    z1, z3 = across(y1, 2), across(y3, 6)
    small = total_over(small, "tensor", (2,))
    small, u_top, u_bottom = together(small, u_top, u_bottom)
    v1, v3 = add_rows(r_near[BLK:], u_top, 0), add_rows(r_far[BLK:], u_bottom, half)
    small, v1, v3 = together(small, v1, v3)
    v1, v3 = swap(v1, 1, 1), swap(v3, 1, 3)
    small = total_over(small, "tensor", (4,))
    small, v1, v3 = together(small, v1, v3)
    small = total_over(small, "tensor", (8,)) * factor
    patch_grad = patch_rows(own_rows, gain, r_near, v1, v3)
    patch_grad, z1, z3 = together(patch_grad, z1, z3)
    weight_grad = weight_out(both, z1, z3, factor)
    shift = small[:, width : 2 * width]
    gain_grad = (small[:, :width] - bias * shift) / gain
    return (
        attention.reshape(1, length, local),
        patch_grad[None],
        weight_grad,
        gain_grad[0],
        shift[0],
        terms[0, :local] * factor,
        terms[0, local:] * factor,
    )


def solution(mesh):
    in_specs = (
        P("dp", "tensor", None),
        P("dp", None),
        P(),
        P(),
        P(None, None, "tensor"),
        P("tensor"),
        P("tensor"),
        P("dp", None, "tensor"),
    )
    out_specs = (
        P("dp", None, "tensor"),
        P("dp", "tensor", None),
        P("dp", None, "tensor"),
        P(),
        P(),
        P("tensor"),
        P("tensor"),
    )
    return jax.shard_map(body, mesh=mesh, in_specs=in_specs, out_specs=out_specs, check_vma=False)
```
